32 devices in a mesh: ctx: 4 (over y, x), tp: 8 (over z, core).
Axes of the slice: x: 2, y: 2, z: 4, core: 2. Of those that a mesh axis runs over, the one named last changes fastest.
Arguments:
- tokens: bfloat16 [512, 16384], P(None, 'ctx'), may hold values from -4 to 4
- wq: bfloat16 [16384, 16384], P('ctx', 'tp'), may hold values from -0.046875 to 0.046875
- wk: bfloat16 [16384, 1024], P('ctx', 'tp'), may hold values from -0.046875 to 0.046875
- wv: bfloat16 [16384, 1024], P('ctx', 'tp'), may hold values from -0.046875 to 0.046875
- doc_len: int32 [16], replicated, may hold values from 1 to 189, as said below
- doc_shard: int32 [16], replicated, may hold values from 0 to 3, as said below
- doc_slot: int32 [16], replicated, may hold values from 0 to 191, as said below
Outputs:
- attended: bfloat16 [768, 16384], P('ctx', 'tp')
The draws below stay inside these ranges and needn't reach their ends.
Inputs may be any that keep to these rules, and one draw needn't show every extreme that they name: `doc_len`: documents lie in the packed sequence in index order and their lengths sum to 512; in every draw some document has length 189. `doc_shard`: each shard holds exactly 4 documents whose lengths sum to at most 192; in every draw some shard holds exactly 192 tokens. The documents of one shard take disjoint runs of slots doc_slot to doc_slot + doc_len - 1, filling the slots from 0 without gaps; in every draw some document starts at slot 191.
All inputs are finite; a program needn't handle non-finite values.
Results may differ from the reference program's by a relative error of at most 0.035.
Values may be sent and summed in bfloat16 or wider, within the bound.
A program may use at most 64 MiB of HBM per device.

```python
import jax
import jax.numpy as jnp
from jax import lax

MODEL_WIDTH = 16384
QUERY_HEADS = 128
KEY_VALUE_HEADS = 8
HEAD_SIZE = 128
TOK_CTX = 128
DPS = 4
SHARD_SLOT_COUNT = 192
TOKENS = 512
SLOT_COUNT_ALL = 768
NDOC = 16
N_CTX = 4


def shard_layout(key):
    keys = jax.random.split(jax.random.fold_in(key, 7), 5)
    pairs = N_CTX // 2
    spare = SHARD_SLOT_COUNT - TOK_CTX
    delta = jax.random.randint(keys[0], (pairs,), 0, spare + 1)
    forced = jax.random.randint(keys[1], (), 0, pairs)
    delta = jnp.where(jnp.arange(pairs) == forced, spare, delta)
    flip = jax.random.randint(keys[2], (pairs,), 0, 2)
    first = TOK_CTX + jnp.where(flip == 1, delta, -delta)
    second = 2 * TOK_CTX - first
    counts = jnp.stack([first, second], axis=1).reshape(N_CTX).astype(jnp.int32)
    raw = jax.random.randint(keys[3], (N_CTX, DPS - 1), 0, 1 << 20)
    raw = raw % (counts[:, None] - DPS + 1)
    cuts = jnp.sort(raw, axis=1) + jnp.arange(1, DPS, dtype=jnp.int32)[None, :]
    full_cuts = (SHARD_SLOT_COUNT - DPS + 1 + jnp.arange(0, DPS - 1, dtype=jnp.int32))[None, :]
    cuts = jnp.where(counts[:, None] == SHARD_SLOT_COUNT, full_cuts, cuts).astype(jnp.int32)
    bounds = jnp.concatenate([jnp.zeros((N_CTX, 1), jnp.int32), cuts, counts[:, None]], axis=1)
    lengths = bounds[:, 1:] - bounds[:, :-1]
    offsets = bounds[:, :-1]
    order = jax.random.permutation(keys[4], NDOC)
    doc_len = lengths.reshape(NDOC)[order].astype(jnp.int32)
    doc_shard = (jnp.arange(NDOC, dtype=jnp.int32) // DPS)[order]
    doc_slot = offsets.reshape(NDOC)[order].astype(jnp.int32)
    return (doc_len, doc_shard, doc_slot)


def draw_doc_len(key, part):
    return shard_layout(key)[0]


def draw_doc_shard(key, part):
    return shard_layout(key)[1]


def draw_doc_slot(key, part):
    return shard_layout(key)[2]


def draw_tokens(key, part):
    keys = jax.random.split(jax.random.fold_in(key, 11), 1)
    values = jnp.clip(jax.random.normal(keys[0], (TOKENS, MODEL_WIDTH), jnp.float32), -4.0, 4.0)
    return values.astype(jnp.bfloat16)


def block_scale(own_key, dims, cuts, smallest, high):
    factor_of, own = 1.0, jax.random.fold_in(own_key, 6)
    for dim, parts in cuts:
        draws = jnp.exp(jax.random.uniform(jax.random.fold_in(own, dim), (parts,), jnp.float32, smallest / len(cuts), high / len(cuts)))
        factor_of = factor_of * jnp.repeat(draws, dims[dim] // parts).reshape([-1 if axis == dim else 1 for axis in range(len(dims))])
    return factor_of


def bell_draw(own_key, shape, scale, reach, pieces=(), kind=jnp.bfloat16):
    array = jax.random.normal(own_key, shape, jnp.float32) * scale
    if len(pieces) > 0:
        array = block_scale(own_key, shape, pieces, -0.22, 0.18) * array
    return jnp.clip(array, min=-reach, max=reach).astype(kind)


def setup_inputs(seed: int = 0) -> dict:
    arg_keys = jax.random.split(jax.random.key(seed), 8)
    return {
        "tokens": draw_tokens(jax.random.fold_in(arg_keys[7], 71), 0),
        "wq": bell_draw(arg_keys[1], (MODEL_WIDTH, QUERY_HEADS * HEAD_SIZE), MODEL_WIDTH ** -0.5, 0.046875, ((0, 4), (1, 8))),
        "wk": bell_draw(arg_keys[2], (MODEL_WIDTH, KEY_VALUE_HEADS * HEAD_SIZE), MODEL_WIDTH ** -0.5, 0.046875, ((0, 4), (1, 8))),
        "wv": bell_draw(arg_keys[3], (MODEL_WIDTH, KEY_VALUE_HEADS * HEAD_SIZE), MODEL_WIDTH ** -0.5, 0.046875, ((0, 4), (1, 8))),
        "doc_len": draw_doc_len(jax.random.fold_in(arg_keys[7], 71), 0),
        "doc_shard": draw_doc_shard(jax.random.fold_in(arg_keys[7], 71), 0),
        "doc_slot": draw_doc_slot(jax.random.fold_in(arg_keys[7], 71), 0),
    }


rope_base = 500000.0


def slot_layout(doc_len, doc_shard, doc_slot, tokens_total, capacity, slot_total):
    ends = jnp.cumsum(doc_len).astype(jnp.int32)
    starts = (ends - doc_len).astype(jnp.int32)
    token_ids = jnp.arange(tokens_total, dtype=jnp.int32)
    inside = (token_ids[:, None] >= starts[None, :]) & (token_ids[:, None] < ends[None, :])
    doc_ids = jnp.arange(doc_len.shape[0], dtype=jnp.int32)
    doc_of = jnp.sum(jnp.where(inside, doc_ids[None, :], 0), axis=1).astype(jnp.int32)
    first = jnp.sum(jnp.where(inside, starts[None, :], 0), axis=1).astype(jnp.int32)
    anchor = (doc_shard * capacity + doc_slot).astype(jnp.int32)
    base = jnp.sum(jnp.where(inside, anchor[None, :], 0), axis=1).astype(jnp.int32)
    position = (token_ids - first).astype(jnp.int32)
    target = (base + position).astype(jnp.int32)
    slot_ids = jnp.arange(slot_total, dtype=jnp.int32)
    source = jnp.zeros((slot_total,), jnp.int32).at[target].set(token_ids)
    filled = jnp.zeros((slot_total,), jnp.int32).at[target].set(1)
    slot_doc = jnp.zeros((slot_total,), jnp.int32).at[target].set(doc_of)
    slot_doc = jnp.where(filled == 1, slot_doc, -1 - slot_ids).astype(jnp.int32)
    slot_position_index = jnp.zeros((slot_total,), jnp.int32).at[target].set(position)
    return source, filled, slot_doc, slot_position_index


def apply_rotary(values, positions):
    head_dim = values.shape[-1]
    half = head_dim // 2
    freq = jnp.power(jnp.float32(rope_base), -jnp.arange(half, dtype=jnp.float32) * (2.0 / head_dim))
    angle = positions.astype(jnp.float32)[:, None] * freq[None, :]
    cosine = jnp.cos(angle)[:, None, :]
    sine = jnp.sin(angle)[:, None, :]
    lower = values[..., :half]
    upper = values[..., half:]
    return jnp.concatenate([lower * cosine - upper * sine, upper * cosine + lower * sine], axis=-1)


def attend(query_matrix, key, value_matrix, slot_doc, slot_position_index):
    scale = query_matrix.shape[-1] ** -0.5
    scores = jnp.einsum("qgjd,kgd->gjqk", query_matrix.astype(jnp.float32), key.astype(jnp.float32)) * scale
    allowed = (slot_doc[:, None] == slot_doc[None, :]) & (slot_position_index[None, :] <= slot_position_index[:, None])
    scores = jnp.where(allowed[None, None], scores, -jnp.inf)
    peak = jnp.max(scores, axis=-1, keepdims=True)
    expo = jnp.exp(scores - peak)
    total = jnp.sum(expo, axis=-1)
    weights = expo.astype(jnp.bfloat16)
    mixed = jnp.einsum("gjqk,kgd->qgjd", weights.astype(jnp.float32), value_matrix.astype(jnp.float32))
    result = mixed / jnp.transpose(total, (2, 0, 1))[..., None]
    return result.astype(jnp.bfloat16)


def reference(tokens, wq, wk, wv, doc_len, doc_shard, doc_slot):
    source, filled, slot_doc, slot_position_index = slot_layout(doc_len, doc_shard, doc_slot, TOKENS, SHARD_SLOT_COUNT, SLOT_COUNT_ALL)
    joined = jnp.concatenate([wq, wk, wv], axis=1)
    width = MODEL_WIDTH // N_CTX
    summed = jnp.zeros((TOKENS, joined.shape[1]), jnp.float32)
    for block in range(N_CTX):
        term = jnp.dot(tokens[:, block * width:(block + 1) * width], joined[block * width:(block + 1) * width], preferred_element_type=jnp.float32).astype(jnp.bfloat16)
        summed = summed + term.astype(jnp.float32)
    projected = jnp.where(filled[:, None] == 1, jnp.take(summed, source, axis=0), jnp.float32(0.0))
    q_cols = QUERY_HEADS * HEAD_SIZE
    key_value_columns = KEY_VALUE_HEADS * HEAD_SIZE
    query_matrix = apply_rotary(projected[:, :q_cols].reshape(SLOT_COUNT_ALL, QUERY_HEADS, HEAD_SIZE), slot_position_index).astype(jnp.bfloat16)
    key_unrotated = lax.optimization_barrier(projected[:, q_cols:q_cols + key_value_columns].astype(jnp.bfloat16))
    value_matrix = projected[:, q_cols + key_value_columns:].astype(jnp.bfloat16)
    key = apply_rotary(key_unrotated.astype(jnp.float32).reshape(SLOT_COUNT_ALL, KEY_VALUE_HEADS, HEAD_SIZE), slot_position_index).astype(jnp.bfloat16)
    query_matrix = query_matrix.reshape(N_CTX, SHARD_SLOT_COUNT, KEY_VALUE_HEADS, QUERY_HEADS // KEY_VALUE_HEADS, HEAD_SIZE)
    key = key.reshape(N_CTX, SHARD_SLOT_COUNT, KEY_VALUE_HEADS, HEAD_SIZE)
    value_matrix = value_matrix.reshape(N_CTX, SHARD_SLOT_COUNT, KEY_VALUE_HEADS, HEAD_SIZE)
    docs = slot_doc.reshape(N_CTX, SHARD_SLOT_COUNT)
    places = slot_position_index.reshape(N_CTX, SHARD_SLOT_COUNT)
    outputs = lax.map(lambda items: attend(items[0], items[1], items[2], items[3], items[4]), (query_matrix, key, value_matrix, docs, places))
    return outputs.reshape(SLOT_COUNT_ALL, QUERY_HEADS * HEAD_SIZE)
```

```python
import functools

import jax
import jax.numpy as jnp
import numpy as np
from jax import lax
from jax.experimental import pallas as pl
from jax.experimental.pallas import tpu as pltpu
from jax.sharding import PartitionSpec as P

HEAD_SIZE = 128


rope_base = 500000.0


def partner(shard, axis, apart):
    return lax.ppermute(shard, axis, [(i, i ^ 1 << apart) for i in range(lax.axis_size(axis))])


def slot_layout(doc_len, doc_shard, doc_slot, tokens_total, capacity, slot_total):
    ends = jnp.cumsum(doc_len)
    starts = ends - doc_len
    token_ids = jnp.arange(tokens_total, dtype=jnp.int32)
    inside = (token_ids[:, None] >= starts[None, :]) & (token_ids[:, None] < ends[None, :])
    doc_ids = jnp.arange(doc_len.shape[0], dtype=jnp.int32)
    doc_of = jnp.sum(jnp.where(inside, doc_ids[None, :], 0), axis=1)
    first = jnp.sum(jnp.where(inside, starts[None, :], 0), axis=1)
    anchor = doc_shard * capacity + doc_slot
    base = jnp.sum(jnp.where(inside, anchor[None, :], 0), axis=1)
    position = token_ids - first
    target = base + position
    slot_ids = jnp.arange(slot_total, dtype=jnp.int32)
    source = jnp.zeros((slot_total,), jnp.int32).at[target].set(token_ids)
    filled = jnp.zeros((slot_total,), jnp.int32).at[target].set(1)
    slot_doc = jnp.zeros((slot_total,), jnp.int32).at[target].set(doc_of)
    slot_doc = jnp.where(filled == 1, slot_doc, -1 - slot_ids)
    slot_position_index = jnp.zeros((slot_total,), jnp.int32).at[target].set(position)
    return (source, filled, slot_doc, slot_position_index)


def apply_rotary(values, positions):
    head_dim = values.shape[-1]
    half = head_dim // 2
    freq = jnp.power(
        jnp.float32(rope_base), -jnp.arange(half, dtype=jnp.float32) * (2.0 / head_dim)
    )
    angle = positions.astype(jnp.float32)[:, None] * freq[None, :]
    cosine = jnp.cos(angle)[:, None, :]
    sine = jnp.sin(angle)[:, None, :]
    lower = values[..., :half]
    upper = values[..., half:]
    return jnp.concatenate([lower * cosine - upper * sine, upper * cosine + lower * sine], axis=-1)


def attend(query_matrix, key, value_matrix, slot_doc, slot_position_index):
    scale = query_matrix.shape[-1] ** (-0.5)
    scores = (
        jnp.einsum("qgjd,kgd->gjqk", query_matrix, key, preferred_element_type=jnp.float32) * scale
    )
    allowed = (slot_doc[:, None] == slot_doc[None, :]) & (
        slot_position_index[None, :] <= slot_position_index[:, None]
    )
    scores = jnp.where(allowed[None, None], scores, -jnp.inf)
    peak = jnp.max(scores, axis=-1, keepdims=True)
    expo = jnp.exp(scores - peak)
    total = jnp.sum(expo, axis=-1)
    weights = expo.astype(jnp.bfloat16)
    mixed = jnp.einsum("gjqk,kgd->qgjd", weights, value_matrix, preferred_element_type=jnp.float32)
    result = mixed / jnp.transpose(total, (2, 0, 1))[..., None]
    return result.astype(jnp.bfloat16)


def plain(tokens, wq, wk, wv, doc_len, doc_shard, doc_slot):
    shards = lax.axis_size("ctx")
    total_tokens = tokens.shape[0]
    per_shard = total_tokens // shards
    capacity = per_shard + per_shard // 2
    slot_total = capacity * shards
    source, filled, slot_doc, slot_position_index = slot_layout(
        doc_len, doc_shard, doc_slot, total_tokens, capacity, slot_total
    )
    joined = jnp.concatenate([wq, wk, wv], axis=1)
    q_cols = wq.shape[1]
    key_value_columns = wk.shape[1]
    picked = jnp.take(tokens, source, axis=0)
    partial_rows = jnp.dot(picked, joined, preferred_element_type=jnp.float32)
    summed = lax.psum_scatter(
        jnp.where(filled[:, None] == 1, partial_rows, jnp.float32(0.0)).astype(jnp.bfloat16),
        "ctx",
        scatter_dimension=0,
        tiled=True,
    ).astype(jnp.float32)
    shard = lax.axis_index("ctx")
    my_doc = lax.dynamic_slice_in_dim(slot_doc, shard * capacity, capacity)
    my_pos = lax.dynamic_slice_in_dim(slot_position_index, shard * capacity, capacity)
    heads_here = q_cols // HEAD_SIZE
    query_matrix = apply_rotary(
        summed[:, :q_cols].reshape(capacity, heads_here, HEAD_SIZE), my_pos
    ).astype(jnp.bfloat16)
    piece = jnp.stack(
        [summed[:, q_cols : q_cols + key_value_columns], summed[:, q_cols + key_value_columns :]],
        axis=0,
    ).astype(jnp.bfloat16)
    members = HEAD_SIZE // key_value_columns
    member = lax.axis_index("tp") % members
    for bit in range(members.bit_length() - 1):
        other = partner(piece, "tp", bit)
        upper_bit = member // 2**bit % 2
        lower_part = jnp.where(upper_bit == 0, piece, other)
        upper_part = jnp.where(upper_bit == 0, other, piece)
        piece = jnp.concatenate([lower_part, upper_part], axis=2)
    key_unrotated = lax.optimization_barrier(piece[0])
    value_matrix = piece[1]
    key = apply_rotary(key_unrotated.astype(jnp.float32)[:, None, :], my_pos).astype(jnp.bfloat16)
    result = attend(
        query_matrix.reshape(capacity, 1, heads_here, HEAD_SIZE),
        key,
        value_matrix[:, None, :],
        my_doc,
        my_pos,
    )
    return result.reshape(capacity, heads_here * HEAD_SIZE)


def fused_kernel(
    shards, capacity, heads_here,
    len_ref, shard_ref, slot_ref, freq_ref, tokens_hbm, wq_hbm, wk_hbm, wv_hbm, out_hbm,
    tok, weights, place, work, inbox, key_buf, value_buf, cos_buf, sin_buf, first_buf, staged,
    tok_sem, w_sem, out_sem, send_sem, recv_sem,
):
    bits = shards.bit_length() - 1
    chunks = heads_here // 2 + 1
    tokens_total = tok.shape[0]
    documents = len_ref.shape[0]
    head = HEAD_SIZE
    lag = 2
    me = lax.axis_index("ctx")
    column = lax.axis_index("tp")
    orders = [list(range(bits)), list(reversed(range(bits)))]
    inbox_at = [sum(shards >> (q + 1) for q in range(p)) * capacity for p in range(bits)]

    def peer(bit):
        step = 1 << bit
        return me + step - 2 * step * ((me // step) % 2)

    def flipped(mask):
        ident = 0
        for bit in range(bits):
            own = (me // (1 << bit)) % 2
            ident = ident + ((1 - own) if (mask >> bit) & 1 else own) * (1 << bit)
        return ident

    def mask_at(order, spot):
        mask = 0
        for p, bit in enumerate(order):
            if (spot >> (bits - 1 - p)) & 1:
                mask |= 1 << bit
        return mask

    def load_key_value():
        return [
            pltpu.make_async_copy(wk_hbm, weights.at[0, :, pl.ds(0, head)], w_sem.at[0]),
            pltpu.make_async_copy(wv_hbm, weights.at[0, :, pl.ds(head, head)], w_sem.at[chunks]),
        ]

    def load_query(c):
        at = pl.multiple_of((c - 1) * (2 * head), 2 * head)
        return pltpu.make_async_copy(
            wq_hbm.at[:, pl.ds(at, 2 * head)], weights.at[c], w_sem.at[c]
        )

    def send(c, half, p):
        rows = (shards >> (p + 1)) * capacity
        return pltpu.make_async_remote_copy(
            src_ref=work.at[c, half, pl.ds(rows, rows)],
            dst_ref=inbox.at[c, half, pl.ds(inbox_at[p], rows)],
            send_sem=send_sem.at[c, half, p],
            recv_sem=recv_sem.at[c, half, p],
            device_id=(peer(orders[half][p]), column),
            device_id_type=pl.DeviceIdType.MESH,
        )

    def store_out(c):
        at = pl.multiple_of((c - 1) * (2 * head), 2 * head)
        return pltpu.make_async_copy(
            staged.at[c], out_hbm.at[:, pl.ds(at, 2 * head)], out_sem.at[c]
        )

    tok_copy = pltpu.make_async_copy(tokens_hbm, tok, tok_sem)
    tok_copy.start()
    for copy in load_key_value():
        copy.start()
    load_query(1).start()

    barrier = pltpu.get_barrier_semaphore()
    for bit in range(bits):
        pl.semaphore_signal(
            barrier, inc=1, device_id=(peer(bit), column), device_id_type=pl.DeviceIdType.MESH
        )

    token_ids = lax.broadcasted_iota(jnp.int32, (1, tokens_total), 1)
    slot_ids = lax.broadcasted_iota(jnp.int32, (capacity, head), 0)

    def place_document(d, carry):
        start, target, first = carry
        length = len_ref[d]
        anchor = shard_ref[d] * capacity + slot_ref[d]
        inside = (token_ids >= start) & (token_ids < start + length)
        target = jnp.where(inside, anchor + token_ids - start, target)
        slot = slot_ref[d]
        here = jnp.where(shard_ref[d] == me, length, 0)
        first = jnp.where((slot_ids >= slot) & (slot_ids < slot + here), slot, first)
        return start + length, target, first

    _, target, first = lax.fori_loop(
        0, documents, place_document, (jnp.int32(0), jnp.zeros_like(token_ids), slot_ids)
    )
    first_buf[...] = first
    local = lax.broadcasted_iota(jnp.int32, (capacity, tokens_total), 0)
    for mask in range(shards):
        hit = local + flipped(mask) * capacity == target
        place[pl.ds(mask * capacity, capacity), :] = jnp.where(hit, 1.0, 0.0).astype(jnp.bfloat16)

    pl.semaphore_wait(barrier, bits)
    tok_copy.wait()

    def produce(c):
        term = jnp.dot(tok[...], weights[c], preferred_element_type=jnp.float32)
        term = term.astype(jnp.bfloat16)
        placed = jnp.dot(place[...], term, preferred_element_type=jnp.float32)
        placed = placed.astype(jnp.bfloat16)
        for half in range(2):
            for spot in reversed(range(shards)):
                mask = mask_at(orders[half], spot)
                work[c, half, pl.ds(spot * capacity, capacity), :] = placed[
                    mask * capacity : (mask + 1) * capacity, half * head : (half + 1) * head
                ]
        for half in range(2):
            send(c, half, 0).start()

    def gathered(c, half, spot, phases):
        value = work[c, half, pl.ds(spot * capacity, capacity), :].astype(jnp.float32)
        for p in range(phases):
            value = value + inbox[
                c, half, pl.ds(inbox_at[p] + spot * capacity, capacity), :
            ].astype(jnp.float32)
        return value

    def relay(c, p):
        for half in range(2):
            send(c, half, p - 1).wait_recv()
            for spot in range(shards >> (p + 1), shards >> p):
                work[c, half, pl.ds(spot * capacity, capacity), :] = gathered(
                    c, half, spot, p
                ).astype(jnp.bfloat16)
            send(c, half, p).start()

    def rotate(value):
        return value * cos_buf[...] + pltpu.roll(value, head // 2, 1) * sin_buf[...]

    def take_key_value():
        for half in range(2):
            send(0, half, bits - 1).wait_recv()
        angle = (slot_ids - first_buf[...]).astype(jnp.float32) * freq_ref[...]
        lane = lax.broadcasted_iota(jnp.int32, (capacity, head), 1)
        cos_buf[...] = jnp.cos(angle)
        sine = jnp.sin(angle)
        sin_buf[...] = jnp.where(lane < head // 2, -sine, sine)
        key_raw = gathered(0, 0, 0, bits).astype(jnp.bfloat16).astype(jnp.float32)
        key_buf[...] = rotate(key_raw).astype(jnp.bfloat16)
        value_buf[...] = gathered(0, 1, 0, bits).astype(jnp.bfloat16)

    def attend_heads(c):
        for half in range(2):
            send(c, half, bits - 1).wait_recv()
        query = jnp.concatenate(
            [rotate(gathered(c, half, 0, bits)).astype(jnp.bfloat16) for half in range(2)], axis=0
        )
        scores = lax.dot_general(
            query, key_buf[...], (((1,), (1,)), ((), ())), preferred_element_type=jnp.float32
        )
        row = lax.broadcasted_iota(jnp.int32, (capacity, capacity), 0)
        col = lax.broadcasted_iota(jnp.int32, (capacity, capacity), 1)
        allowed = (col <= row) & (col >= first_buf[:, :1])
        allowed = jnp.concatenate([allowed, allowed], axis=0)
        scores = jnp.where(allowed, scores * (head**-0.5), -jnp.inf)
        peak = jnp.max(scores, axis=-1, keepdims=True)
        expo = jnp.exp(scores - peak)
        total = jnp.sum(expo, axis=-1, keepdims=True)
        mixed = jnp.dot(
            expo.astype(jnp.bfloat16), value_buf[...], preferred_element_type=jnp.float32
        )
        result = (mixed / total).astype(jnp.bfloat16)
        for half in range(2):
            staged[c, :, half * head : (half + 1) * head] = result[
                half * capacity : (half + 1) * capacity
            ]
        store_out(c).start()

    def step(c, _):
        @pl.when(c == 0)
        def _():
            for copy in load_key_value():
                copy.wait()

        @pl.when((c > 0) & (c < chunks))
        def _():
            load_query(c).wait()

        @pl.when(c + 2 < chunks)
        def _():
            load_query(c + 2).start()

        @pl.when(c < chunks)
        def _():
            produce(c)

        for p in range(1, bits):
            @pl.when((c >= lag * p) & (c < chunks + lag * p))
            def _():
                relay(c - lag * p, p)

        @pl.when(c == lag * bits)
        def _():
            take_key_value()

        @pl.when(c > lag * bits)
        def _():
            attend_heads(c - lag * bits)

        return 0

    lax.fori_loop(0, chunks + lag * bits, step, 0)

    def finish(c, _):
        for half in range(2):
            for p in range(bits):
                send(c, half, p).wait_send()

        @pl.when(c > 0)
        def _():
            store_out(c).wait()

        return 0

    lax.fori_loop(0, chunks, finish, 0)


def fused(tokens, wq, wk, wv, doc_len, doc_shard, doc_slot):
    shards = lax.axis_size("ctx")
    bits = shards.bit_length() - 1
    total_tokens, depth = tokens.shape
    per_shard = total_tokens // shards
    capacity = per_shard + per_shard // 2
    q_cols = wq.shape[1]
    heads_here = q_cols // HEAD_SIZE
    chunks = heads_here // 2 + 1
    half = HEAD_SIZE // 2
    freq = np.power(np.float32(rope_base), -np.arange(half, dtype=np.float32) * np.float32(2.0 / HEAD_SIZE))
    freq = jnp.asarray(np.tile(freq, 2)[None, :], jnp.float32)
    smem = pl.BlockSpec(memory_space=pltpu.SMEM)
    hbm = pl.BlockSpec(memory_space=pl.ANY)
    bf16 = jnp.bfloat16
    return pl.pallas_call(
        functools.partial(fused_kernel, shards, capacity, heads_here),
        out_shape=jax.ShapeDtypeStruct((capacity, q_cols), bf16),
        in_specs=[smem, smem, smem, pl.BlockSpec(memory_space=pltpu.VMEM), hbm, hbm, hbm, hbm],
        out_specs=hbm,
        scratch_shapes=[
            pltpu.VMEM((total_tokens, depth), bf16),
            pltpu.VMEM((chunks, depth, 2 * HEAD_SIZE), bf16),
            pltpu.VMEM((shards * capacity, total_tokens), bf16),
            pltpu.VMEM((chunks, 2, shards * capacity, HEAD_SIZE), bf16),
            pltpu.VMEM((chunks, 2, (shards - 1) * capacity, HEAD_SIZE), bf16),
            pltpu.VMEM((capacity, HEAD_SIZE), bf16),
            pltpu.VMEM((capacity, HEAD_SIZE), bf16),
            pltpu.VMEM((capacity, HEAD_SIZE), jnp.float32),
            pltpu.VMEM((capacity, HEAD_SIZE), jnp.float32),
            pltpu.VMEM((capacity, HEAD_SIZE), jnp.int32),
            pltpu.VMEM((chunks, capacity, 2 * HEAD_SIZE), bf16),
            pltpu.SemaphoreType.DMA,
            pltpu.SemaphoreType.DMA((chunks + 1,)),
            pltpu.SemaphoreType.DMA((chunks,)),
            pltpu.SemaphoreType.DMA((chunks, 2, bits)),
            pltpu.SemaphoreType.DMA((chunks, 2, bits)),
        ],
        compiler_params=pltpu.CompilerParams(
            collective_id=0, has_side_effects=True, vmem_limit_bytes=56 * 2**20
        ),
        cost_estimate=pl.CostEstimate(
            flops=2 * total_tokens * depth * (q_cols + 2 * HEAD_SIZE),
            bytes_accessed=2 * depth * (total_tokens + q_cols + 2 * HEAD_SIZE),
            transcendentals=0,
        ),
    )(doc_len, doc_shard, doc_slot, freq, tokens, wq, wk, wv)


def body(tokens, wq, wk, wv, doc_len, doc_shard, doc_slot):
    shards = lax.axis_size("ctx")
    if wk.shape[1] == HEAD_SIZE and shards & (shards - 1) == 0:
        return fused(tokens, wq, wk, wv, doc_len, doc_shard, doc_slot)
    return plain(tokens, wq, wk, wv, doc_len, doc_shard, doc_slot)


def solution(mesh):
    return jax.shard_map(
        body,
        mesh=mesh,
        in_specs=(P(None, "ctx"), P("ctx", "tp"), P("ctx", "tp"), P("ctx", "tp"), P(), P(), P()),
        out_specs=P("ctx", "tp"),
        check_vma=False,
    )
```

```python
import functools

import jax
import jax.numpy as jnp
import numpy as np
from jax import lax
from jax.experimental import pallas as pl
from jax.experimental.pallas import tpu as pltpu
from jax.sharding import PartitionSpec as P

HEAD_SIZE = 128


rope_base = 500000.0


def partner(shard, axis, apart):
    return lax.ppermute(shard, axis, [(i, i ^ 1 << apart) for i in range(lax.axis_size(axis))])


def slot_layout(doc_len, doc_shard, doc_slot, tokens_total, capacity, slot_total):
    ends = jnp.cumsum(doc_len)
    starts = ends - doc_len
    token_ids = jnp.arange(tokens_total, dtype=jnp.int32)
    inside = (token_ids[:, None] >= starts[None, :]) & (token_ids[:, None] < ends[None, :])
    doc_ids = jnp.arange(doc_len.shape[0], dtype=jnp.int32)
    doc_of = jnp.sum(jnp.where(inside, doc_ids[None, :], 0), axis=1)
    first = jnp.sum(jnp.where(inside, starts[None, :], 0), axis=1)
    anchor = doc_shard * capacity + doc_slot
    base = jnp.sum(jnp.where(inside, anchor[None, :], 0), axis=1)
    position = token_ids - first
    target = base + position
    slot_ids = jnp.arange(slot_total, dtype=jnp.int32)
    source = jnp.zeros((slot_total,), jnp.int32).at[target].set(token_ids)
    filled = jnp.zeros((slot_total,), jnp.int32).at[target].set(1)
    slot_doc = jnp.zeros((slot_total,), jnp.int32).at[target].set(doc_of)
    slot_doc = jnp.where(filled == 1, slot_doc, -1 - slot_ids)
    slot_position_index = jnp.zeros((slot_total,), jnp.int32).at[target].set(position)
    return (source, filled, slot_doc, slot_position_index)


def apply_rotary(values, positions):
    head_dim = values.shape[-1]
    half = head_dim // 2
    freq = jnp.power(
        jnp.float32(rope_base), -jnp.arange(half, dtype=jnp.float32) * (2.0 / head_dim)
    )
    angle = positions.astype(jnp.float32)[:, None] * freq[None, :]
    cosine = jnp.cos(angle)[:, None, :]
    sine = jnp.sin(angle)[:, None, :]
    lower = values[..., :half]
    upper = values[..., half:]
    return jnp.concatenate([lower * cosine - upper * sine, upper * cosine + lower * sine], axis=-1)


def attend(query_matrix, key, value_matrix, slot_doc, slot_position_index):
    scale = query_matrix.shape[-1] ** (-0.5)
    scores = (
        jnp.einsum("qgjd,kgd->gjqk", query_matrix, key, preferred_element_type=jnp.float32) * scale
    )
    allowed = (slot_doc[:, None] == slot_doc[None, :]) & (
        slot_position_index[None, :] <= slot_position_index[:, None]
    )
    scores = jnp.where(allowed[None, None], scores, -jnp.inf)
    peak = jnp.max(scores, axis=-1, keepdims=True)
    expo = jnp.exp(scores - peak)
    total = jnp.sum(expo, axis=-1)
    weights = expo.astype(jnp.bfloat16)
    mixed = jnp.einsum("gjqk,kgd->qgjd", weights, value_matrix, preferred_element_type=jnp.float32)
    result = mixed / jnp.transpose(total, (2, 0, 1))[..., None]
    return result.astype(jnp.bfloat16)


def plain(tokens, wq, wk, wv, doc_len, doc_shard, doc_slot):
    shards = lax.axis_size("ctx")
    total_tokens = tokens.shape[0]
    per_shard = total_tokens // shards
    capacity = per_shard + per_shard // 2
    slot_total = capacity * shards
    source, filled, slot_doc, slot_position_index = slot_layout(
        doc_len, doc_shard, doc_slot, total_tokens, capacity, slot_total
    )
    joined = jnp.concatenate([wq, wk, wv], axis=1)
    q_cols = wq.shape[1]
    key_value_columns = wk.shape[1]
    picked = jnp.take(tokens, source, axis=0)
    partial_rows = jnp.dot(picked, joined, preferred_element_type=jnp.float32)
    summed = lax.psum_scatter(
        jnp.where(filled[:, None] == 1, partial_rows, jnp.float32(0.0)).astype(jnp.bfloat16),
        "ctx",
        scatter_dimension=0,
        tiled=True,
    ).astype(jnp.float32)
    shard = lax.axis_index("ctx")
    my_doc = lax.dynamic_slice_in_dim(slot_doc, shard * capacity, capacity)
    my_pos = lax.dynamic_slice_in_dim(slot_position_index, shard * capacity, capacity)
    heads_here = q_cols // HEAD_SIZE
    query_matrix = apply_rotary(
        summed[:, :q_cols].reshape(capacity, heads_here, HEAD_SIZE), my_pos
    ).astype(jnp.bfloat16)
    piece = jnp.stack(
        [summed[:, q_cols : q_cols + key_value_columns], summed[:, q_cols + key_value_columns :]],
        axis=0,
    ).astype(jnp.bfloat16)
    members = HEAD_SIZE // key_value_columns
    member = lax.axis_index("tp") % members
    for bit in range(members.bit_length() - 1):
        other = partner(piece, "tp", bit)
        upper_bit = member // 2**bit % 2
        lower_part = jnp.where(upper_bit == 0, piece, other)
        upper_part = jnp.where(upper_bit == 0, other, piece)
        piece = jnp.concatenate([lower_part, upper_part], axis=2)
    key_unrotated = lax.optimization_barrier(piece[0])
    value_matrix = piece[1]
    key = apply_rotary(key_unrotated.astype(jnp.float32)[:, None, :], my_pos).astype(jnp.bfloat16)
    result = attend(
        query_matrix.reshape(capacity, 1, heads_here, HEAD_SIZE),
        key,
        value_matrix[:, None, :],
        my_doc,
        my_pos,
    )
    return result.reshape(capacity, heads_here * HEAD_SIZE)


def fused_kernel(
    shards, capacity, heads_here,
    len_hbm, shard_hbm, slot_hbm, freq_hbm, tokens_hbm, wq_hbm, wk_hbm, wv_hbm, out_ref,
    len_ref, shard_ref, slot_ref, freq_ref, tok, weights, place, work, inbox, total_buf, term_buf,
    key_buf, value_buf, cos_buf, sin_buf, first_buf,
    table_sem, piece_sem, w_sem, send_sem, recv_sem,
):
    bits = shards.bit_length() - 1
    chunks = heads_here // 2 + 1
    tokens_total, depth = tok.shape
    pieces = piece_sem.shape[0]
    piece = depth // pieces
    documents = len_ref.shape[0]
    head = HEAD_SIZE
    lag = 2
    me = lax.axis_index("ctx")
    column = lax.axis_index("tp")
    orders = [list(range(bits)), list(reversed(range(bits)))]
    inbox_at = [sum(shards >> (q + 1) for q in range(p)) * capacity for p in range(bits)]

    def peer(bit):
        step = 1 << bit
        return me + step - 2 * step * ((me // step) % 2)

    def flipped(mask):
        ident = 0
        for bit in range(bits):
            own = (me // (1 << bit)) % 2
            ident = ident + ((1 - own) if (mask >> bit) & 1 else own) * (1 << bit)
        return ident

    def mask_at(order, spot):
        mask = 0
        for p, bit in enumerate(order):
            if (spot >> (bits - 1 - p)) & 1:
                mask |= 1 << bit
        return mask

    tables = [
        pltpu.make_async_copy(source, target, table_sem.at[i])
        for i, (source, target) in enumerate(
            [(len_hbm, len_ref), (shard_hbm, shard_ref), (slot_hbm, slot_ref), (freq_hbm, freq_ref)]
        )
    ]

    def load_piece(k):
        part = pl.ds(pl.multiple_of(k * piece, piece), piece)
        return [
            pltpu.make_async_copy(tokens_hbm.at[:, part], tok.at[:, part], piece_sem.at[k, 0]),
            pltpu.make_async_copy(
                wk_hbm.at[part], weights.at[0, part, pl.ds(0, head)], piece_sem.at[k, 1]
            ),
            pltpu.make_async_copy(
                wv_hbm.at[part], weights.at[0, part, pl.ds(head, head)], piece_sem.at[k, 2]
            ),
        ]

    def load_query(c):
        at = pl.multiple_of((c - 1) * (2 * head), 2 * head)
        return pltpu.make_async_copy(
            wq_hbm.at[:, pl.ds(at, 2 * head)], weights.at[c], w_sem.at[c]
        )

    def send(c, half, p):
        rows = (shards >> (p + 1)) * capacity
        return pltpu.make_async_remote_copy(
            src_ref=work.at[c, half, pl.ds(rows, rows)],
            dst_ref=inbox.at[c, half, pl.ds(inbox_at[p], rows)],
            send_sem=send_sem.at[c, half, p],
            recv_sem=recv_sem.at[c, half, p],
            device_id=(peer(orders[half][p]), column),
            device_id_type=pl.DeviceIdType.MESH,
        )

    for copy in tables:
        copy.start()
    for k in range(pieces):
        for copy in load_piece(k):
            copy.start()

    barrier = pltpu.get_barrier_semaphore()
    for bit in range(bits):
        pl.semaphore_signal(
            barrier, inc=1, device_id=(peer(bit), column), device_id_type=pl.DeviceIdType.MESH
        )

    token_ids = lax.broadcasted_iota(jnp.int32, (1, tokens_total), 1)
    slot_ids = lax.broadcasted_iota(jnp.int32, (capacity, head), 0)

    for copy in tables:
        copy.wait()

    def place_document(d, carry):
        start, target, first = carry
        length = len_ref[d]
        anchor = shard_ref[d] * capacity + slot_ref[d]
        inside = (token_ids >= start) & (token_ids < start + length)
        target = jnp.where(inside, anchor + token_ids - start, target)
        slot = slot_ref[d]
        here = jnp.where(shard_ref[d] == me, length, 0)
        first = jnp.where((slot_ids >= slot) & (slot_ids < slot + here), slot, first)
        return start + length, target, first

    _, target, first = lax.fori_loop(
        0, documents, place_document, (jnp.int32(0), jnp.zeros_like(token_ids), slot_ids)
    )
    first_buf[...] = first
    local = lax.broadcasted_iota(jnp.int32, (capacity, tokens_total), 0)
    for mask in range(shards):
        hit = local + flipped(mask) * capacity == target
        place[pl.ds(mask * capacity, capacity), :] = jnp.where(hit, 1.0, 0.0).astype(jnp.bfloat16)

    def first_product():
        total_buf[...] = jnp.zeros_like(total_buf)

        def add_piece(k, _):
            for copy in load_piece(k):
                copy.wait()
            part = pl.ds(pl.multiple_of(k * piece, piece), piece)
            total_buf[...] += jnp.dot(
                tok[:, part], weights[0, part, :], preferred_element_type=jnp.float32
            )
            return 0

        lax.fori_loop(0, pieces - 1, add_piece, 0)
        load_query(1).start()
        add_piece(pieces - 1, 0)
        term_buf[...] = total_buf[...].astype(jnp.bfloat16)
        pl.semaphore_wait(barrier, bits)

    def product(c):
        load_query(c).wait()
        term_buf[...] = jnp.dot(
            tok[...], weights[c], preferred_element_type=jnp.float32
        ).astype(jnp.bfloat16)

    def produce(c):
        placed = jnp.dot(place[...], term_buf[...], preferred_element_type=jnp.float32)
        placed = placed.astype(jnp.bfloat16)
        for half in range(2):
            for spot in reversed(range(shards)):
                mask = mask_at(orders[half], spot)
                work[c, half, pl.ds(spot * capacity, capacity), :] = placed[
                    mask * capacity : (mask + 1) * capacity, half * head : (half + 1) * head
                ]
        for half in range(2):
            send(c, half, 0).start()

    def gathered(c, half, spot, phases):
        value = work[c, half, pl.ds(spot * capacity, capacity), :].astype(jnp.float32)
        for p in range(phases):
            value = value + inbox[
                c, half, pl.ds(inbox_at[p] + spot * capacity, capacity), :
            ].astype(jnp.float32)
        return value

    def relay(c, p):
        for half in range(2):
            send(c, half, p - 1).wait_recv()
            for spot in range(shards >> (p + 1), shards >> p):
                work[c, half, pl.ds(spot * capacity, capacity), :] = gathered(
                    c, half, spot, p
                ).astype(jnp.bfloat16)
            send(c, half, p).start()

    def rotate(value):
        return value * cos_buf[...] + pltpu.roll(value, head // 2, 1) * sin_buf[...]

    def take_key_value():
        for half in range(2):
            send(0, half, bits - 1).wait_recv()
        angle = (slot_ids - first_buf[...]).astype(jnp.float32) * freq_ref[...]
        lane = lax.broadcasted_iota(jnp.int32, (capacity, head), 1)
        cos_buf[...] = jnp.cos(angle)
        sine = jnp.sin(angle)
        sin_buf[...] = jnp.where(lane < head // 2, -sine, sine)
        key_raw = gathered(0, 0, 0, bits).astype(jnp.bfloat16).astype(jnp.float32)
        key_buf[...] = rotate(key_raw).astype(jnp.bfloat16)
        value_buf[...] = gathered(0, 1, 0, bits).astype(jnp.bfloat16)

    def attend_heads(c):
        for half in range(2):
            send(c, half, bits - 1).wait_recv()
        query = jnp.concatenate(
            [rotate(gathered(c, half, 0, bits)).astype(jnp.bfloat16) for half in range(2)], axis=0
        )
        scores = lax.dot_general(
            query, key_buf[...], (((1,), (1,)), ((), ())), preferred_element_type=jnp.float32
        )
        row = lax.broadcasted_iota(jnp.int32, (capacity, capacity), 0)
        col = lax.broadcasted_iota(jnp.int32, (capacity, capacity), 1)
        allowed = (col <= row) & (col >= first_buf[:, :1])
        allowed = jnp.concatenate([allowed, allowed], axis=0)
        scores = jnp.where(allowed, scores, -jnp.inf)
        peak = jnp.max(scores, axis=-1, keepdims=True)
        expo = jnp.exp2((scores - peak) * (head**-0.5 * np.log2(np.e)))
        total = jnp.sum(expo, axis=-1, keepdims=True)
        mixed = jnp.dot(
            expo.astype(jnp.bfloat16), value_buf[...], preferred_element_type=jnp.float32
        )
        result = (mixed / total).astype(jnp.bfloat16)
        for half in range(2):
            at = pl.multiple_of((c - 1) * (2 * head) + half * head, head)
            out_ref[:, pl.ds(at, head)] = result[half * capacity : (half + 1) * capacity]

    def step(c, _):
        @pl.when(c == 0)
        def _():
            first_product()

        @pl.when((c > 0) & (c < chunks))
        def _():
            product(c)

        @pl.when(c + 2 < chunks)
        def _():
            load_query(c + 2).start()

        @pl.when(c < chunks)
        def _():
            produce(c)

        for p in range(1, bits):
            @pl.when((c >= lag * p) & (c < chunks + lag * p))
            def _():
                relay(c - lag * p, p)

        @pl.when(c == lag * bits)
        def _():
            take_key_value()

        @pl.when(c > lag * bits)
        def _():
            attend_heads(c - lag * bits)

        return 0

    lax.fori_loop(0, chunks + lag * bits, step, 0)

    def finish(c, _):
        for half in range(2):
            for p in range(bits):
                send(c, half, p).wait_send()
        return 0

    lax.fori_loop(0, chunks, finish, 0)


def fused(tokens, wq, wk, wv, doc_len, doc_shard, doc_slot):
    shards = lax.axis_size("ctx")
    bits = shards.bit_length() - 1
    total_tokens, depth = tokens.shape
    per_shard = total_tokens // shards
    capacity = per_shard + per_shard // 2
    q_cols = wq.shape[1]
    heads_here = q_cols // HEAD_SIZE
    chunks = heads_here // 2 + 1
    half = HEAD_SIZE // 2
    freq = np.power(np.float32(rope_base), -np.arange(half, dtype=np.float32) * np.float32(2.0 / HEAD_SIZE))
    freq = jnp.asarray(np.tile(freq, 2)[None, :], jnp.float32)
    documents = doc_len.shape[0]
    hbm = pl.BlockSpec(memory_space=pl.ANY)
    bf16 = jnp.bfloat16
    return pl.pallas_call(
        functools.partial(fused_kernel, shards, capacity, heads_here),
        out_shape=pltpu.VMEM((capacity, q_cols), bf16),
        in_specs=[hbm] * 8,
        out_specs=pl.BlockSpec(memory_space=pltpu.VMEM),
        scratch_shapes=[
            pltpu.SMEM((documents,), jnp.int32),
            pltpu.SMEM((documents,), jnp.int32),
            pltpu.SMEM((documents,), jnp.int32),
            pltpu.VMEM((1, HEAD_SIZE), jnp.float32),
            pltpu.VMEM((total_tokens, depth), bf16),
            pltpu.VMEM((chunks, depth, 2 * HEAD_SIZE), bf16),
            pltpu.VMEM((shards * capacity, total_tokens), bf16),
            pltpu.VMEM((chunks, 2, shards * capacity, HEAD_SIZE), bf16),
            pltpu.VMEM((chunks, 2, (shards - 1) * capacity, HEAD_SIZE), bf16),
            pltpu.VMEM((total_tokens, 2 * HEAD_SIZE), jnp.float32),
            pltpu.VMEM((total_tokens, 2 * HEAD_SIZE), bf16),
            pltpu.VMEM((capacity, HEAD_SIZE), bf16),
            pltpu.VMEM((capacity, HEAD_SIZE), bf16),
            pltpu.VMEM((capacity, HEAD_SIZE), jnp.float32),
            pltpu.VMEM((capacity, HEAD_SIZE), jnp.float32),
            pltpu.VMEM((capacity, HEAD_SIZE), jnp.int32),
            pltpu.SemaphoreType.DMA((4,)),
            pltpu.SemaphoreType.DMA((4, 3)),
            pltpu.SemaphoreType.DMA((chunks,)),
            pltpu.SemaphoreType.DMA((chunks, 2, bits)),
            pltpu.SemaphoreType.DMA((chunks, 2, bits)),
        ],
        compiler_params=pltpu.CompilerParams(
            collective_id=0, has_side_effects=True, vmem_limit_bytes=56 * 2**20
        ),
        cost_estimate=pl.CostEstimate(
            flops=2 * total_tokens * depth * (q_cols + 2 * HEAD_SIZE),
            bytes_accessed=2 * depth * (total_tokens + q_cols + 2 * HEAD_SIZE),
            transcendentals=0,
        ),
    )(doc_len, doc_shard, doc_slot, freq, tokens, wq, wk, wv)


def body(tokens, wq, wk, wv, doc_len, doc_shard, doc_slot):
    shards = lax.axis_size("ctx")
    if wk.shape[1] == HEAD_SIZE and shards & (shards - 1) == 0:
        return fused(tokens, wq, wk, wv, doc_len, doc_shard, doc_slot)
    return plain(tokens, wq, wk, wv, doc_len, doc_shard, doc_slot)


def solution(mesh):
    return jax.shard_map(
        body,
        mesh=mesh,
        in_specs=(P(None, "ctx"), P("ctx", "tp"), P("ctx", "tp"), P("ctx", "tp"), P(), P(), P()),
        out_specs=P("ctx", "tp"),
        check_vma=False,
    )
```

```python
import functools

import jax
import jax.numpy as jnp
import numpy as np
from jax import lax
from jax.experimental import pallas as pl
from jax.experimental.pallas import tpu as pltpu
from jax.sharding import PartitionSpec as P

HEAD_SIZE = 128


rope_base = 500000.0


def partner(shard, axis, apart):
    return lax.ppermute(shard, axis, [(i, i ^ 1 << apart) for i in range(lax.axis_size(axis))])


def slot_layout(doc_len, doc_shard, doc_slot, tokens_total, capacity, slot_total):
    ends = jnp.cumsum(doc_len)
    starts = ends - doc_len
    token_ids = jnp.arange(tokens_total, dtype=jnp.int32)
    inside = (token_ids[:, None] >= starts[None, :]) & (token_ids[:, None] < ends[None, :])
    doc_ids = jnp.arange(doc_len.shape[0], dtype=jnp.int32)
    doc_of = jnp.sum(jnp.where(inside, doc_ids[None, :], 0), axis=1)
    first = jnp.sum(jnp.where(inside, starts[None, :], 0), axis=1)
    anchor = doc_shard * capacity + doc_slot
    base = jnp.sum(jnp.where(inside, anchor[None, :], 0), axis=1)
    position = token_ids - first
    target = base + position
    slot_ids = jnp.arange(slot_total, dtype=jnp.int32)
    source = jnp.zeros((slot_total,), jnp.int32).at[target].set(token_ids)
    filled = jnp.zeros((slot_total,), jnp.int32).at[target].set(1)
    slot_doc = jnp.zeros((slot_total,), jnp.int32).at[target].set(doc_of)
    slot_doc = jnp.where(filled == 1, slot_doc, -1 - slot_ids)
    slot_position_index = jnp.zeros((slot_total,), jnp.int32).at[target].set(position)
    return (source, filled, slot_doc, slot_position_index)


def apply_rotary(values, positions):
    head_dim = values.shape[-1]
    half = head_dim // 2
    freq = jnp.power(
        jnp.float32(rope_base), -jnp.arange(half, dtype=jnp.float32) * (2.0 / head_dim)
    )
    angle = positions.astype(jnp.float32)[:, None] * freq[None, :]
    cosine = jnp.cos(angle)[:, None, :]
    sine = jnp.sin(angle)[:, None, :]
    lower = values[..., :half]
    upper = values[..., half:]
    return jnp.concatenate([lower * cosine - upper * sine, upper * cosine + lower * sine], axis=-1)


def attend(query_matrix, key, value_matrix, slot_doc, slot_position_index):
    scale = query_matrix.shape[-1] ** (-0.5)
    scores = (
        jnp.einsum("qgjd,kgd->gjqk", query_matrix, key, preferred_element_type=jnp.float32) * scale
    )
    allowed = (slot_doc[:, None] == slot_doc[None, :]) & (
        slot_position_index[None, :] <= slot_position_index[:, None]
    )
    scores = jnp.where(allowed[None, None], scores, -jnp.inf)
    peak = jnp.max(scores, axis=-1, keepdims=True)
    expo = jnp.exp(scores - peak)
    total = jnp.sum(expo, axis=-1)
    weights = expo.astype(jnp.bfloat16)
    mixed = jnp.einsum("gjqk,kgd->qgjd", weights, value_matrix, preferred_element_type=jnp.float32)
    result = mixed / jnp.transpose(total, (2, 0, 1))[..., None]
    return result.astype(jnp.bfloat16)


def plain(tokens, wq, wk, wv, doc_len, doc_shard, doc_slot):
    shards = lax.axis_size("ctx")
    total_tokens = tokens.shape[0]
    per_shard = total_tokens // shards
    capacity = per_shard + per_shard // 2
    slot_total = capacity * shards
    source, filled, slot_doc, slot_position_index = slot_layout(
        doc_len, doc_shard, doc_slot, total_tokens, capacity, slot_total
    )
    joined = jnp.concatenate([wq, wk, wv], axis=1)
    q_cols = wq.shape[1]
    key_value_columns = wk.shape[1]
    picked = jnp.take(tokens, source, axis=0)
    partial_rows = jnp.dot(picked, joined, preferred_element_type=jnp.float32)
    summed = lax.psum_scatter(
        jnp.where(filled[:, None] == 1, partial_rows, jnp.float32(0.0)).astype(jnp.bfloat16),
        "ctx",
        scatter_dimension=0,
        tiled=True,
    ).astype(jnp.float32)
    shard = lax.axis_index("ctx")
    my_doc = lax.dynamic_slice_in_dim(slot_doc, shard * capacity, capacity)
    my_pos = lax.dynamic_slice_in_dim(slot_position_index, shard * capacity, capacity)
    heads_here = q_cols // HEAD_SIZE
    query_matrix = apply_rotary(
        summed[:, :q_cols].reshape(capacity, heads_here, HEAD_SIZE), my_pos
    ).astype(jnp.bfloat16)
    piece = jnp.stack(
        [summed[:, q_cols : q_cols + key_value_columns], summed[:, q_cols + key_value_columns :]],
        axis=0,
    ).astype(jnp.bfloat16)
    members = HEAD_SIZE // key_value_columns
    member = lax.axis_index("tp") % members
    for bit in range(members.bit_length() - 1):
        other = partner(piece, "tp", bit)
        upper_bit = member // 2**bit % 2
        lower_part = jnp.where(upper_bit == 0, piece, other)
        upper_part = jnp.where(upper_bit == 0, other, piece)
        piece = jnp.concatenate([lower_part, upper_part], axis=2)
    key_unrotated = lax.optimization_barrier(piece[0])
    value_matrix = piece[1]
    key = apply_rotary(key_unrotated.astype(jnp.float32)[:, None, :], my_pos).astype(jnp.bfloat16)
    result = attend(
        query_matrix.reshape(capacity, 1, heads_here, HEAD_SIZE),
        key,
        value_matrix[:, None, :],
        my_doc,
        my_pos,
    )
    return result.reshape(capacity, heads_here * HEAD_SIZE)


def fused_kernel(
    shards, capacity, heads_here,
    len_hbm, shard_hbm, slot_hbm, freq_hbm, tokens_hbm, wq_hbm, wk_hbm, wv_hbm, out_ref,
    len_ref, shard_ref, slot_ref, freq_ref, tok, weights, place, work, inbox, total_buf, term_buf,
    key_buf, value_buf, cos_buf, sin_buf, first_buf, mask_buf,
    table_sem, piece_sem, w_sem, send_sem, recv_sem,
):
    bits = shards.bit_length() - 1
    chunks = heads_here // 2 + 1
    tokens_total, depth = tok.shape
    pieces = piece_sem.shape[0]
    piece = depth // pieces
    documents = len_ref.shape[0]
    head = HEAD_SIZE
    lag = 2
    me = lax.axis_index("ctx")
    column = lax.axis_index("tp")
    orders = [list(range(bits)), list(reversed(range(bits)))]
    inbox_at = [sum(shards >> (q + 1) for q in range(p)) * capacity for p in range(bits)]

    def peer(bit):
        step = 1 << bit
        return me + step - 2 * step * ((me // step) % 2)

    def flipped(mask):
        ident = 0
        for bit in range(bits):
            own = (me // (1 << bit)) % 2
            ident = ident + ((1 - own) if (mask >> bit) & 1 else own) * (1 << bit)
        return ident

    def mask_at(order, spot):
        mask = 0
        for p, bit in enumerate(order):
            if (spot >> (bits - 1 - p)) & 1:
                mask |= 1 << bit
        return mask

    tables = [
        pltpu.make_async_copy(source, target, table_sem.at[i])
        for i, (source, target) in enumerate(
            [(len_hbm, len_ref), (shard_hbm, shard_ref), (slot_hbm, slot_ref), (freq_hbm, freq_ref)]
        )
    ]

    def load_piece(k):
        part = pl.ds(pl.multiple_of(k * piece, piece), piece)
        return [
            pltpu.make_async_copy(tokens_hbm.at[:, part], tok.at[:, part], piece_sem.at[k, 0]),
            pltpu.make_async_copy(
                wk_hbm.at[part], weights.at[0, part, pl.ds(0, head)], piece_sem.at[k, 1]
            ),
            pltpu.make_async_copy(
                wv_hbm.at[part], weights.at[0, part, pl.ds(head, head)], piece_sem.at[k, 2]
            ),
        ]

    def load_query(c):
        at = pl.multiple_of((c - 1) * (2 * head), 2 * head)
        return pltpu.make_async_copy(
            wq_hbm.at[:, pl.ds(at, 2 * head)], weights.at[c], w_sem.at[c]
        )

    def send(c, half, p):
        rows = (shards >> (p + 1)) * capacity
        return pltpu.make_async_remote_copy(
            src_ref=work.at[c, half, pl.ds(rows, rows)],
            dst_ref=inbox.at[c, half, pl.ds(inbox_at[p], rows)],
            send_sem=send_sem.at[c, half, p],
            recv_sem=recv_sem.at[c, half, p],
            device_id=(peer(orders[half][p]), column),
            device_id_type=pl.DeviceIdType.MESH,
        )

    for copy in tables:
        copy.start()
    for k in range(pieces):
        for copy in load_piece(k):
            copy.start()

    barrier = pltpu.get_barrier_semaphore()
    for bit in range(bits):
        pl.semaphore_signal(
            barrier, inc=1, device_id=(peer(bit), column), device_id_type=pl.DeviceIdType.MESH
        )

    token_ids = lax.broadcasted_iota(jnp.int32, (1, tokens_total), 1)
    slot_ids = lax.broadcasted_iota(jnp.int32, (capacity, head), 0)

    for copy in tables:
        copy.wait()

    def place_document(d, carry):
        start, target, first = carry
        length = len_ref[d]
        anchor = shard_ref[d] * capacity + slot_ref[d]
        inside = (token_ids >= start) & (token_ids < start + length)
        target = jnp.where(inside, anchor + token_ids - start, target)
        slot = slot_ref[d]
        here = jnp.where(shard_ref[d] == me, length, 0)
        first = jnp.where((slot_ids >= slot) & (slot_ids < slot + here), slot, first)
        return start + length, target, first

    _, target, first = lax.fori_loop(
        0, documents, place_document, (jnp.int32(0), jnp.zeros_like(token_ids), slot_ids)
    )
    first_buf[...] = first
    local = lax.broadcasted_iota(jnp.int32, (capacity, tokens_total), 0)
    for mask in range(shards):
        hit = local + flipped(mask) * capacity == target
        place[pl.ds(mask * capacity, capacity), :] = jnp.where(hit, 1.0, 0.0).astype(jnp.bfloat16)

    def first_product():
        total_buf[...] = jnp.zeros_like(total_buf)

        def add_piece(k, _):
            for copy in load_piece(k):
                copy.wait()
            part = pl.ds(pl.multiple_of(k * piece, piece), piece)
            total_buf[...] += jnp.dot(
                tok[:, part], weights[0, part, :], preferred_element_type=jnp.float32
            )
            return 0

        lax.fori_loop(0, pieces - 1, add_piece, 0)
        load_query(1).start()
        add_piece(pieces - 1, 0)
        term_buf[...] = total_buf[...].astype(jnp.bfloat16)
        pl.semaphore_wait(barrier, bits)

    def product(c):
        load_query(c).wait()
        term_buf[...] = jnp.dot(
            tok[...], weights[c], preferred_element_type=jnp.float32
        ).astype(jnp.bfloat16)

    def produce(c):
        placed = jnp.dot(place[...], term_buf[...], preferred_element_type=jnp.float32)
        placed = placed.astype(jnp.bfloat16)
        for half in range(2):
            for spot in reversed(range(shards)):
                mask = mask_at(orders[half], spot)
                work[c, half, pl.ds(spot * capacity, capacity), :] = placed[
                    mask * capacity : (mask + 1) * capacity, half * head : (half + 1) * head
                ]
        for half in range(2):
            send(c, half, 0).start()

    def gathered(c, half, spot, phases):
        value = work[c, half, pl.ds(spot * capacity, capacity), :].astype(jnp.float32)
        for p in range(phases):
            value = value + inbox[
                c, half, pl.ds(inbox_at[p] + spot * capacity, capacity), :
            ].astype(jnp.float32)
        return value

    def relay(c, p):
        for half in range(2):
            send(c, half, p - 1).wait_recv()
            for spot in range(shards >> (p + 1), shards >> p):
                work[c, half, pl.ds(spot * capacity, capacity), :] = gathered(
                    c, half, spot, p
                ).astype(jnp.bfloat16)
            send(c, half, p).start()

    def rotate(value):
        return value * cos_buf[...] + pltpu.roll(value, head // 2, 1) * sin_buf[...]

    def take_key_value():
        wait_last(0)
        angle = (slot_ids - first_buf[...]).astype(jnp.float32) * freq_ref[...]
        lane = lax.broadcasted_iota(jnp.int32, (capacity, head), 1)
        cos_buf[...] = jnp.cos(angle)
        sine = jnp.sin(angle)
        sin_buf[...] = jnp.where(lane < head // 2, -sine, sine)
        key_raw = gathered(0, 0, 0, bits).astype(jnp.bfloat16).astype(jnp.float32)
        key_buf[...] = rotate(key_raw).astype(jnp.bfloat16)
        value_buf[:, :head] = gathered(0, 1, 0, bits).astype(jnp.bfloat16)
        value_buf[:, head:] = jnp.ones((capacity, head), jnp.bfloat16)
        row = lax.broadcasted_iota(jnp.int32, (capacity, capacity), 0)
        col = lax.broadcasted_iota(jnp.int32, (capacity, capacity), 1)
        allowed = (col <= row) & (col >= first_buf[:, :1])
        mask_buf[...] = jnp.where(allowed, 0.0, -jnp.inf)

    def attend_heads(c):
        query = [rotate(gathered(c, half, 0, bits)).astype(jnp.bfloat16) for half in range(2)]
        for low in range(0, capacity, head):
            high = min(low + head, capacity)
            rows = high - low
            scores = lax.dot_general(
                jnp.concatenate([q[low:high] for q in query], axis=0),
                key_buf[:high],
                (((1,), (1,)), ((), ())),
                preferred_element_type=jnp.float32,
            )
            mask = mask_buf[low:high, :high]
            scores = scores + jnp.concatenate([mask, mask], axis=0)
            peak = jnp.max(scores, axis=-1, keepdims=True)
            expo = jnp.exp2((scores - peak) * (head**-0.5 * np.log2(np.e)))
            mixed = jnp.dot(
                expo.astype(jnp.bfloat16), value_buf[:high], preferred_element_type=jnp.float32
            )
            result = (mixed[:, :head] / mixed[:, head:]).astype(jnp.bfloat16)
            for half in range(2):
                at = pl.multiple_of((c - 1) * (2 * head) + half * head, head)
                out_ref[low:high, pl.ds(at, head)] = result[half * rows : (half + 1) * rows]

    def wait_last(c):
        for half in range(2):
            send(c, half, bits - 1).wait_recv()

    def step(c, _):
        @pl.when(c == 0)
        def _():
            first_product()

        @pl.when((c > 0) & (c < chunks))
        def _():
            product(c)

        @pl.when(c + 2 < chunks)
        def _():
            load_query(c + 2).start()

        @pl.when(c < chunks)
        def _():
            produce(c)

        for p in range(1, bits):
            @pl.when((c >= lag * p) & (c < chunks + lag * p))
            def _():
                relay(c - lag * p, p)

        @pl.when(c == lag * bits)
        def _():
            take_key_value()

        @pl.when(c > lag * bits)
        def _():
            wait_last(c - lag * bits)
            attend_heads(c - lag * bits)

        return 0

    def steady_step(c, _):
        for p in reversed(range(1, bits)):
            relay(c - lag * p, p)
        wait_last(c - lag * bits)
        load_query(c).wait()
        term = jnp.dot(tok[...], weights[c], preferred_element_type=jnp.float32)
        attend_heads(c - lag * bits)
        term_buf[...] = term.astype(jnp.bfloat16)
        produce(c)

        @pl.when(c + 2 < chunks)
        def _():
            load_query(c + 2).start()

        return 0

    begin = min(lag * bits + 1, chunks)
    lax.fori_loop(0, begin, step, 0)
    lax.fori_loop(begin, chunks, steady_step, 0)
    lax.fori_loop(chunks, chunks + lag * bits, step, 0)

    def finish(c, _):
        for half in range(2):
            for p in range(bits):
                send(c, half, p).wait_send()
        return 0

    lax.fori_loop(0, chunks, finish, 0)


def fused(tokens, wq, wk, wv, doc_len, doc_shard, doc_slot):
    shards = lax.axis_size("ctx")
    bits = shards.bit_length() - 1
    total_tokens, depth = tokens.shape
    per_shard = total_tokens // shards
    capacity = per_shard + per_shard // 2
    q_cols = wq.shape[1]
    heads_here = q_cols // HEAD_SIZE
    chunks = heads_here // 2 + 1
    half = HEAD_SIZE // 2
    freq = np.power(np.float32(rope_base), -np.arange(half, dtype=np.float32) * np.float32(2.0 / HEAD_SIZE))
    freq = jnp.asarray(np.tile(freq, 2)[None, :], jnp.float32)
    documents = doc_len.shape[0]
    hbm = pl.BlockSpec(memory_space=pl.ANY)
    bf16 = jnp.bfloat16
    return pl.pallas_call(
        functools.partial(fused_kernel, shards, capacity, heads_here),
        out_shape=pltpu.VMEM((capacity, q_cols), bf16),
        in_specs=[hbm] * 8,
        out_specs=pl.BlockSpec(memory_space=pltpu.VMEM),
        scratch_shapes=[
            pltpu.SMEM((documents,), jnp.int32),
            pltpu.SMEM((documents,), jnp.int32),
            pltpu.SMEM((documents,), jnp.int32),
            pltpu.VMEM((1, HEAD_SIZE), jnp.float32),
            pltpu.VMEM((total_tokens, depth), bf16),
            pltpu.VMEM((chunks, depth, 2 * HEAD_SIZE), bf16),
            pltpu.VMEM((shards * capacity, total_tokens), bf16),
            pltpu.VMEM((chunks, 2, shards * capacity, HEAD_SIZE), bf16),
            pltpu.VMEM((chunks, 2, (shards - 1) * capacity, HEAD_SIZE), bf16),
            pltpu.VMEM((total_tokens, 2 * HEAD_SIZE), jnp.float32),
            pltpu.VMEM((total_tokens, 2 * HEAD_SIZE), bf16),
            pltpu.VMEM((capacity, HEAD_SIZE), bf16),
            pltpu.VMEM((capacity, 2 * HEAD_SIZE), bf16),
            pltpu.VMEM((capacity, HEAD_SIZE), jnp.float32),
            pltpu.VMEM((capacity, HEAD_SIZE), jnp.float32),
            pltpu.VMEM((capacity, HEAD_SIZE), jnp.int32),
            pltpu.VMEM((capacity, capacity), jnp.float32),
            pltpu.SemaphoreType.DMA((4,)),
            pltpu.SemaphoreType.DMA((4, 3)),
            pltpu.SemaphoreType.DMA((chunks,)),
            pltpu.SemaphoreType.DMA((chunks, 2, bits)),
            pltpu.SemaphoreType.DMA((chunks, 2, bits)),
        ],
        compiler_params=pltpu.CompilerParams(
            collective_id=0, has_side_effects=True, vmem_limit_bytes=56 * 2**20
        ),
        cost_estimate=pl.CostEstimate(
            flops=2 * total_tokens * depth * (q_cols + 2 * HEAD_SIZE),
            bytes_accessed=2 * depth * (total_tokens + q_cols + 2 * HEAD_SIZE),
            transcendentals=0,
        ),
    )(doc_len, doc_shard, doc_slot, freq, tokens, wq, wk, wv)


def body(tokens, wq, wk, wv, doc_len, doc_shard, doc_slot):
    shards = lax.axis_size("ctx")
    if wk.shape[1] == HEAD_SIZE and shards & (shards - 1) == 0:
        return fused(tokens, wq, wk, wv, doc_len, doc_shard, doc_slot)
    return plain(tokens, wq, wk, wv, doc_len, doc_shard, doc_slot)


def solution(mesh):
    return jax.shard_map(
        body,
        mesh=mesh,
        in_specs=(P(None, "ctx"), P("ctx", "tp"), P("ctx", "tp"), P("ctx", "tp"), P(), P(), P()),
        out_specs=P("ctx", "tp"),
        check_vma=False,
    )
```

```python
import functools

import jax
import jax.numpy as jnp
import numpy as np
from jax import lax
from jax.experimental import pallas as pl
from jax.experimental.pallas import tpu as pltpu
from jax.sharding import PartitionSpec as P

HEAD_SIZE = 128


rope_base = 500000.0


def partner(shard, axis, apart):
    return lax.ppermute(shard, axis, [(i, i ^ 1 << apart) for i in range(lax.axis_size(axis))])


def slot_layout(doc_len, doc_shard, doc_slot, tokens_total, capacity, slot_total):
    ends = jnp.cumsum(doc_len)
    starts = ends - doc_len
    token_ids = jnp.arange(tokens_total, dtype=jnp.int32)
    inside = (token_ids[:, None] >= starts[None, :]) & (token_ids[:, None] < ends[None, :])
    doc_ids = jnp.arange(doc_len.shape[0], dtype=jnp.int32)
    doc_of = jnp.sum(jnp.where(inside, doc_ids[None, :], 0), axis=1)
    first = jnp.sum(jnp.where(inside, starts[None, :], 0), axis=1)
    anchor = doc_shard * capacity + doc_slot
    base = jnp.sum(jnp.where(inside, anchor[None, :], 0), axis=1)
    position = token_ids - first
    target = base + position
    slot_ids = jnp.arange(slot_total, dtype=jnp.int32)
    source = jnp.zeros((slot_total,), jnp.int32).at[target].set(token_ids)
    filled = jnp.zeros((slot_total,), jnp.int32).at[target].set(1)
    slot_doc = jnp.zeros((slot_total,), jnp.int32).at[target].set(doc_of)
    slot_doc = jnp.where(filled == 1, slot_doc, -1 - slot_ids)
    slot_position_index = jnp.zeros((slot_total,), jnp.int32).at[target].set(position)
    return (source, filled, slot_doc, slot_position_index)


def apply_rotary(values, positions):
    head_dim = values.shape[-1]
    half = head_dim // 2
    freq = jnp.power(
        jnp.float32(rope_base), -jnp.arange(half, dtype=jnp.float32) * (2.0 / head_dim)
    )
    angle = positions.astype(jnp.float32)[:, None] * freq[None, :]
    cosine = jnp.cos(angle)[:, None, :]
    sine = jnp.sin(angle)[:, None, :]
    lower = values[..., :half]
    upper = values[..., half:]
    return jnp.concatenate([lower * cosine - upper * sine, upper * cosine + lower * sine], axis=-1)


def attend(query_matrix, key, value_matrix, slot_doc, slot_position_index):
    scale = query_matrix.shape[-1] ** (-0.5)
    scores = (
        jnp.einsum("qgjd,kgd->gjqk", query_matrix, key, preferred_element_type=jnp.float32) * scale
    )
    allowed = (slot_doc[:, None] == slot_doc[None, :]) & (
        slot_position_index[None, :] <= slot_position_index[:, None]
    )
    scores = jnp.where(allowed[None, None], scores, -jnp.inf)
    peak = jnp.max(scores, axis=-1, keepdims=True)
    expo = jnp.exp(scores - peak)
    total = jnp.sum(expo, axis=-1)
    weights = expo.astype(jnp.bfloat16)
    mixed = jnp.einsum("gjqk,kgd->qgjd", weights, value_matrix, preferred_element_type=jnp.float32)
    result = mixed / jnp.transpose(total, (2, 0, 1))[..., None]
    return result.astype(jnp.bfloat16)


def plain(tokens, wq, wk, wv, doc_len, doc_shard, doc_slot):
    shards = lax.axis_size("ctx")
    total_tokens = tokens.shape[0]
    per_shard = total_tokens // shards
    capacity = per_shard + per_shard // 2
    slot_total = capacity * shards
    source, filled, slot_doc, slot_position_index = slot_layout(
        doc_len, doc_shard, doc_slot, total_tokens, capacity, slot_total
    )
    joined = jnp.concatenate([wq, wk, wv], axis=1)
    q_cols = wq.shape[1]
    key_value_columns = wk.shape[1]
    picked = jnp.take(tokens, source, axis=0)
    partial_rows = jnp.dot(picked, joined, preferred_element_type=jnp.float32)
    summed = lax.psum_scatter(
        jnp.where(filled[:, None] == 1, partial_rows, jnp.float32(0.0)).astype(jnp.bfloat16),
        "ctx",
        scatter_dimension=0,
        tiled=True,
    ).astype(jnp.float32)
    shard = lax.axis_index("ctx")
    my_doc = lax.dynamic_slice_in_dim(slot_doc, shard * capacity, capacity)
    my_pos = lax.dynamic_slice_in_dim(slot_position_index, shard * capacity, capacity)
    heads_here = q_cols // HEAD_SIZE
    query_matrix = apply_rotary(
        summed[:, :q_cols].reshape(capacity, heads_here, HEAD_SIZE), my_pos
    ).astype(jnp.bfloat16)
    piece = jnp.stack(
        [summed[:, q_cols : q_cols + key_value_columns], summed[:, q_cols + key_value_columns :]],
        axis=0,
    ).astype(jnp.bfloat16)
    members = HEAD_SIZE // key_value_columns
    member = lax.axis_index("tp") % members
    for bit in range(members.bit_length() - 1):
        other = partner(piece, "tp", bit)
        upper_bit = member // 2**bit % 2
        lower_part = jnp.where(upper_bit == 0, piece, other)
        upper_part = jnp.where(upper_bit == 0, other, piece)
        piece = jnp.concatenate([lower_part, upper_part], axis=2)
    key_unrotated = lax.optimization_barrier(piece[0])
    value_matrix = piece[1]
    key = apply_rotary(key_unrotated.astype(jnp.float32)[:, None, :], my_pos).astype(jnp.bfloat16)
    result = attend(
        query_matrix.reshape(capacity, 1, heads_here, HEAD_SIZE),
        key,
        value_matrix[:, None, :],
        my_doc,
        my_pos,
    )
    return result.reshape(capacity, heads_here * HEAD_SIZE)


def fused_kernel(
    shards, capacity, heads_here,
    len_hbm, shard_hbm, slot_hbm, freq_hbm, tokens_hbm, wq_hbm, wk_hbm, wv_hbm, out_ref,
    len_ref, shard_ref, slot_ref, freq_ref, tok, weights, place, work, inbox, total_buf, term_buf,
    key_buf, value_buf, cos_buf, sin_buf, first_buf, mask_buf,
    table_sem, piece_sem, w_sem, send_sem, recv_sem,
):
    bits = shards.bit_length() - 1
    chunks = heads_here // 2 + 1
    tokens_total, depth = tok.shape
    pieces = piece_sem.shape[0]
    piece = depth // pieces
    documents = len_ref.shape[0]
    head = HEAD_SIZE
    lags = [2 * p + 1 for p in range(bits + 1)]
    last_lag = lags[bits]
    me = lax.axis_index("ctx")
    column = lax.axis_index("tp")
    orders = [list(range(bits)), list(reversed(range(bits)))]
    inbox_at = [sum(shards >> (q + 1) for q in range(p)) * capacity for p in range(bits)]

    def peer(bit):
        step = 1 << bit
        return me + step - 2 * step * ((me // step) % 2)

    def flipped(mask):
        ident = 0
        for bit in range(bits):
            own = (me // (1 << bit)) % 2
            ident = ident + ((1 - own) if (mask >> bit) & 1 else own) * (1 << bit)
        return ident

    def mask_at(order, spot):
        mask = 0
        for p, bit in enumerate(order):
            if (spot >> (bits - 1 - p)) & 1:
                mask |= 1 << bit
        return mask

    tables = [
        pltpu.make_async_copy(source, target, table_sem.at[i])
        for i, (source, target) in enumerate(
            [(len_hbm, len_ref), (shard_hbm, shard_ref), (slot_hbm, slot_ref), (freq_hbm, freq_ref)]
        )
    ]

    def load_piece(k):
        part = pl.ds(k * piece, piece)
        return [
            pltpu.make_async_copy(tokens_hbm.at[:, part], tok.at[:, part], piece_sem.at[k, 0]),
            pltpu.make_async_copy(
                wk_hbm.at[part], weights.at[0, part, pl.ds(0, head)], piece_sem.at[k, 1]
            ),
            pltpu.make_async_copy(
                wv_hbm.at[part], weights.at[0, part, pl.ds(head, head)], piece_sem.at[k, 2]
            ),
        ]

    def load_query(c):
        at = pl.multiple_of((c - 1) * (2 * head), 2 * head)
        return pltpu.make_async_copy(
            wq_hbm.at[:, pl.ds(at, 2 * head)], weights.at[c], w_sem.at[c]
        )

    def send(c, half, p):
        rows = (shards >> (p + 1)) * capacity
        return pltpu.make_async_remote_copy(
            src_ref=work.at[c, half, pl.ds(rows, rows)],
            dst_ref=inbox.at[c, half, pl.ds(inbox_at[p], rows)],
            send_sem=send_sem.at[c, half, p],
            recv_sem=recv_sem.at[c, half, p],
            device_id=(peer(orders[half][p]), column),
            device_id_type=pl.DeviceIdType.MESH,
        )

    for copy in tables:
        copy.start()
    for k in range(pieces):
        for copy in load_piece(k):
            copy.start()

    barrier = pltpu.get_barrier_semaphore()
    for bit in range(bits):
        pl.semaphore_signal(
            barrier, inc=1, device_id=(peer(bit), column), device_id_type=pl.DeviceIdType.MESH
        )

    token_ids = lax.broadcasted_iota(jnp.int32, (1, tokens_total), 1)
    slot_ids = lax.broadcasted_iota(jnp.int32, (capacity, head), 0)

    for copy in tables:
        copy.wait()

    def place_document(d, carry):
        start, target = carry
        length = len_ref[d]
        anchor = shard_ref[d] * capacity + slot_ref[d]
        inside = (token_ids >= start) & (token_ids < start + length)
        target = jnp.where(inside, anchor + token_ids - start, target)
        return start + length, target

    _, target = lax.fori_loop(
        0, documents, place_document, (jnp.int32(0), jnp.zeros_like(token_ids))
    )

    def build_place():
        local = lax.broadcasted_iota(jnp.int32, (capacity, tokens_total), 0)
        for mask in range(shards):
            hit = local == target - flipped(mask) * capacity
            place[pl.ds(mask * capacity, capacity), :] = jnp.where(hit, 1.0, 0.0).astype(
                jnp.bfloat16
            )

    def first_slot(d, first):
        slot = slot_ref[d]
        here = jnp.where(shard_ref[d] == me, len_ref[d], 0)
        return jnp.where((slot_ids >= slot) & (slot_ids < slot + here), slot, first)

    def first_product():
        for k in range(pieces):
            if k == pieces - 1:
                load_query(1).start()
                build_place()
            for copy in load_piece(k):
                copy.wait()
            part = pl.ds(k * piece, piece)
            term = jnp.dot(
                tok[:, part], weights[0, part, :], preferred_element_type=jnp.float32
            )
            if k > 0:
                term = total_buf[...] + term
            if k < pieces - 1:
                total_buf[...] = term
        term_buf[...] = term.astype(jnp.bfloat16)
        pl.semaphore_wait(barrier, bits)

    def product(c):
        load_query(c).wait()
        term_buf[...] = jnp.dot(
            tok[...], weights[c], preferred_element_type=jnp.float32
        ).astype(jnp.bfloat16)

    def produce(c):
        placed = jnp.dot(place[...], term_buf[...], preferred_element_type=jnp.float32)
        placed = placed.astype(jnp.bfloat16)
        for half in range(2):
            for spot in reversed(range(shards)):
                mask = mask_at(orders[half], spot)
                work[c, half, pl.ds(spot * capacity, capacity), :] = placed[
                    mask * capacity : (mask + 1) * capacity, half * head : (half + 1) * head
                ]
        for half in range(2):
            send(c, half, 0).start()

    def gathered(c, half, spot, phases):
        value = work[c, half, pl.ds(spot * capacity, capacity), :].astype(jnp.float32)
        for p in range(phases):
            value = value + inbox[
                c, half, pl.ds(inbox_at[p] + spot * capacity, capacity), :
            ].astype(jnp.float32)
        return value

    def relay(c, p):
        for half in range(2):
            send(c, half, p - 1).wait_recv()
            for spot in range(shards >> (p + 1), shards >> p):
                work[c, half, pl.ds(spot * capacity, capacity), :] = gathered(
                    c, half, spot, p
                ).astype(jnp.bfloat16)
            send(c, half, p).start()

    def rotate(value):
        return value * cos_buf[...] + pltpu.roll(value, head // 2, 1) * sin_buf[...]

    def take_key_value():
        wait_last(0)
        first = lax.fori_loop(0, documents, first_slot, slot_ids)
        first_buf[...] = first
        angle = (slot_ids - first).astype(jnp.float32) * freq_ref[...]
        lane = lax.broadcasted_iota(jnp.int32, (capacity, head), 1)
        cos_buf[...] = jnp.cos(angle)
        sine = jnp.sin(angle)
        sin_buf[...] = jnp.where(lane < head // 2, -sine, sine)
        key_raw = gathered(0, 0, 0, bits).astype(jnp.bfloat16).astype(jnp.float32)
        key_buf[...] = rotate(key_raw).astype(jnp.bfloat16)
        value_buf[:, :head] = gathered(0, 1, 0, bits).astype(jnp.bfloat16)
        value_buf[:, head:] = jnp.ones((capacity, head), jnp.bfloat16)
        row = lax.broadcasted_iota(jnp.int32, (capacity, capacity), 0)
        col = lax.broadcasted_iota(jnp.int32, (capacity, capacity), 1)
        allowed = (col <= row) & (col >= first_buf[:, :1])
        mask_buf[...] = jnp.where(allowed, 0.0, -jnp.inf)

    def attend_heads(c):
        query = [rotate(gathered(c, half, 0, bits)).astype(jnp.bfloat16) for half in range(2)]
        for low in range(0, capacity, head):
            high = min(low + head, capacity)
            rows = high - low
            scores = lax.dot_general(
                jnp.concatenate([q[low:high] for q in query], axis=0),
                key_buf[:high],
                (((1,), (1,)), ((), ())),
                preferred_element_type=jnp.float32,
            )
            mask = mask_buf[low:high, :high]
            scores = scores + jnp.concatenate([mask, mask], axis=0)
            peak = jnp.max(scores, axis=-1, keepdims=True)
            expo = jnp.exp2((scores - peak) * (head**-0.5 * np.log2(np.e)))
            mixed = jnp.dot(
                expo.astype(jnp.bfloat16), value_buf[:high], preferred_element_type=jnp.float32
            )
            result = (mixed[:, :head] / mixed[:, head:]).astype(jnp.bfloat16)
            for half in range(2):
                at = pl.multiple_of((c - 1) * (2 * head) + half * head, head)
                out_ref[low:high, pl.ds(at, head)] = result[half * rows : (half + 1) * rows]

    def wait_last(c):
        for half in range(2):
            send(c, half, bits - 1).wait_recv()

    def step(c, _):
        @pl.when(c == 0)
        def _():
            first_product()

        @pl.when((c > 0) & (c < chunks))
        def _():
            product(c)

        @pl.when(c + 2 < chunks)
        def _():
            load_query(c + 2).start()

        @pl.when(c < chunks)
        def _():
            produce(c)

        for p in range(1, bits):
            @pl.when((c >= lags[p]) & (c < chunks + lags[p]))
            def _():
                relay(c - lags[p], p)

        @pl.when(c == last_lag)
        def _():
            take_key_value()

        @pl.when(c > last_lag)
        def _():
            wait_last(c - last_lag)
            attend_heads(c - last_lag)

        return 0

    lax.fori_loop(0, chunks + last_lag, step, 0)

    def finish(c, _):
        for half in range(2):
            for p in range(bits):
                send(c, half, p).wait_send()
        return 0

    lax.fori_loop(0, chunks, finish, 0)


def fused(tokens, wq, wk, wv, doc_len, doc_shard, doc_slot):
    shards = lax.axis_size("ctx")
    bits = shards.bit_length() - 1
    total_tokens, depth = tokens.shape
    per_shard = total_tokens // shards
    capacity = per_shard + per_shard // 2
    q_cols = wq.shape[1]
    heads_here = q_cols // HEAD_SIZE
    chunks = heads_here // 2 + 1
    half = HEAD_SIZE // 2
    freq = np.power(np.float32(rope_base), -np.arange(half, dtype=np.float32) * np.float32(2.0 / HEAD_SIZE))
    freq = jnp.asarray(np.tile(freq, 2)[None, :], jnp.float32)
    documents = doc_len.shape[0]
    hbm = pl.BlockSpec(memory_space=pl.ANY)
    bf16 = jnp.bfloat16
    return pl.pallas_call(
        functools.partial(fused_kernel, shards, capacity, heads_here),
        out_shape=pltpu.VMEM((capacity, q_cols), bf16),
        in_specs=[hbm] * 8,
        out_specs=pl.BlockSpec(memory_space=pltpu.VMEM),
        scratch_shapes=[
            pltpu.SMEM((documents,), jnp.int32),
            pltpu.SMEM((documents,), jnp.int32),
            pltpu.SMEM((documents,), jnp.int32),
            pltpu.VMEM((1, HEAD_SIZE), jnp.float32),
            pltpu.VMEM((total_tokens, depth), bf16),
            pltpu.VMEM((chunks, depth, 2 * HEAD_SIZE), bf16),
            pltpu.VMEM((shards * capacity, total_tokens), bf16),
            pltpu.VMEM((chunks, 2, shards * capacity, HEAD_SIZE), bf16),
            pltpu.VMEM((chunks, 2, (shards - 1) * capacity, HEAD_SIZE), bf16),
            pltpu.VMEM((total_tokens, 2 * HEAD_SIZE), jnp.float32),
            pltpu.VMEM((total_tokens, 2 * HEAD_SIZE), bf16),
            pltpu.VMEM((capacity, HEAD_SIZE), bf16),
            pltpu.VMEM((capacity, 2 * HEAD_SIZE), bf16),
            pltpu.VMEM((capacity, HEAD_SIZE), jnp.float32),
            pltpu.VMEM((capacity, HEAD_SIZE), jnp.float32),
            pltpu.VMEM((capacity, HEAD_SIZE), jnp.int32),
            pltpu.VMEM((capacity, capacity), jnp.float32),
            pltpu.SemaphoreType.DMA((4,)),
            pltpu.SemaphoreType.DMA((4, 3)),
            pltpu.SemaphoreType.DMA((chunks,)),
            pltpu.SemaphoreType.DMA((chunks, 2, bits)),
            pltpu.SemaphoreType.DMA((chunks, 2, bits)),
        ],
        compiler_params=pltpu.CompilerParams(
            collective_id=0, has_side_effects=True, vmem_limit_bytes=56 * 2**20
        ),
        cost_estimate=pl.CostEstimate(
            flops=2 * total_tokens * depth * (q_cols + 2 * HEAD_SIZE),
            bytes_accessed=2 * depth * (total_tokens + q_cols + 2 * HEAD_SIZE),
            transcendentals=0,
        ),
    )(doc_len, doc_shard, doc_slot, freq, tokens, wq, wk, wv)


def body(tokens, wq, wk, wv, doc_len, doc_shard, doc_slot):
    shards = lax.axis_size("ctx")
    if wk.shape[1] == HEAD_SIZE and shards & (shards - 1) == 0:
        return fused(tokens, wq, wk, wv, doc_len, doc_shard, doc_slot)
    return plain(tokens, wq, wk, wv, doc_len, doc_shard, doc_slot)


def solution(mesh):
    return jax.shard_map(
        body,
        mesh=mesh,
        in_specs=(P(None, "ctx"), P("ctx", "tp"), P("ctx", "tp"), P("ctx", "tp"), P(), P(), P()),
        out_specs=P("ctx", "tp"),
        check_vma=False,
    )
```

```python
import functools

import jax
import jax.numpy as jnp
import numpy as np
from jax import lax
from jax.experimental import pallas as pl
from jax.experimental.pallas import tpu as pltpu
from jax.sharding import PartitionSpec as P

HEAD_SIZE = 128


rope_base = 500000.0


def partner(shard, axis, apart):
    return lax.ppermute(shard, axis, [(i, i ^ 1 << apart) for i in range(lax.axis_size(axis))])


def slot_layout(doc_len, doc_shard, doc_slot, tokens_total, capacity, slot_total):
    ends = jnp.cumsum(doc_len)
    starts = ends - doc_len
    token_ids = jnp.arange(tokens_total, dtype=jnp.int32)
    inside = (token_ids[:, None] >= starts[None, :]) & (token_ids[:, None] < ends[None, :])
    doc_ids = jnp.arange(doc_len.shape[0], dtype=jnp.int32)
    doc_of = jnp.sum(jnp.where(inside, doc_ids[None, :], 0), axis=1)
    first = jnp.sum(jnp.where(inside, starts[None, :], 0), axis=1)
    anchor = doc_shard * capacity + doc_slot
    base = jnp.sum(jnp.where(inside, anchor[None, :], 0), axis=1)
    position = token_ids - first
    target = base + position
    slot_ids = jnp.arange(slot_total, dtype=jnp.int32)
    source = jnp.zeros((slot_total,), jnp.int32).at[target].set(token_ids)
    filled = jnp.zeros((slot_total,), jnp.int32).at[target].set(1)
    slot_doc = jnp.zeros((slot_total,), jnp.int32).at[target].set(doc_of)
    slot_doc = jnp.where(filled == 1, slot_doc, -1 - slot_ids)
    slot_position_index = jnp.zeros((slot_total,), jnp.int32).at[target].set(position)
    return (source, filled, slot_doc, slot_position_index)


def apply_rotary(values, positions):
    head_dim = values.shape[-1]
    half = head_dim // 2
    freq = jnp.power(
        jnp.float32(rope_base), -jnp.arange(half, dtype=jnp.float32) * (2.0 / head_dim)
    )
    angle = positions.astype(jnp.float32)[:, None] * freq[None, :]
    cosine = jnp.cos(angle)[:, None, :]
    sine = jnp.sin(angle)[:, None, :]
    lower = values[..., :half]
    upper = values[..., half:]
    return jnp.concatenate([lower * cosine - upper * sine, upper * cosine + lower * sine], axis=-1)


def attend(query_matrix, key, value_matrix, slot_doc, slot_position_index):
    scale = query_matrix.shape[-1] ** (-0.5)
    scores = (
        jnp.einsum("qgjd,kgd->gjqk", query_matrix, key, preferred_element_type=jnp.float32) * scale
    )
    allowed = (slot_doc[:, None] == slot_doc[None, :]) & (
        slot_position_index[None, :] <= slot_position_index[:, None]
    )
    scores = jnp.where(allowed[None, None], scores, -jnp.inf)
    peak = jnp.max(scores, axis=-1, keepdims=True)
    expo = jnp.exp(scores - peak)
    total = jnp.sum(expo, axis=-1)
    weights = expo.astype(jnp.bfloat16)
    mixed = jnp.einsum("gjqk,kgd->qgjd", weights, value_matrix, preferred_element_type=jnp.float32)
    result = mixed / jnp.transpose(total, (2, 0, 1))[..., None]
    return result.astype(jnp.bfloat16)


def plain(tokens, wq, wk, wv, doc_len, doc_shard, doc_slot):
    shards = lax.axis_size("ctx")
    total_tokens = tokens.shape[0]
    per_shard = total_tokens // shards
    capacity = per_shard + per_shard // 2
    slot_total = capacity * shards
    source, filled, slot_doc, slot_position_index = slot_layout(
        doc_len, doc_shard, doc_slot, total_tokens, capacity, slot_total
    )
    joined = jnp.concatenate([wq, wk, wv], axis=1)
    q_cols = wq.shape[1]
    key_value_columns = wk.shape[1]
    picked = jnp.take(tokens, source, axis=0)
    partial_rows = jnp.dot(picked, joined, preferred_element_type=jnp.float32)
    summed = lax.psum_scatter(
        jnp.where(filled[:, None] == 1, partial_rows, jnp.float32(0.0)).astype(jnp.bfloat16),
        "ctx",
        scatter_dimension=0,
        tiled=True,
    ).astype(jnp.float32)
    shard = lax.axis_index("ctx")
    my_doc = lax.dynamic_slice_in_dim(slot_doc, shard * capacity, capacity)
    my_pos = lax.dynamic_slice_in_dim(slot_position_index, shard * capacity, capacity)
    heads_here = q_cols // HEAD_SIZE
    query_matrix = apply_rotary(
        summed[:, :q_cols].reshape(capacity, heads_here, HEAD_SIZE), my_pos
    ).astype(jnp.bfloat16)
    piece = jnp.stack(
        [summed[:, q_cols : q_cols + key_value_columns], summed[:, q_cols + key_value_columns :]],
        axis=0,
    ).astype(jnp.bfloat16)
    members = HEAD_SIZE // key_value_columns
    member = lax.axis_index("tp") % members
    for bit in range(members.bit_length() - 1):
        other = partner(piece, "tp", bit)
        upper_bit = member // 2**bit % 2
        lower_part = jnp.where(upper_bit == 0, piece, other)
        upper_part = jnp.where(upper_bit == 0, other, piece)
        piece = jnp.concatenate([lower_part, upper_part], axis=2)
    key_unrotated = lax.optimization_barrier(piece[0])
    value_matrix = piece[1]
    key = apply_rotary(key_unrotated.astype(jnp.float32)[:, None, :], my_pos).astype(jnp.bfloat16)
    result = attend(
        query_matrix.reshape(capacity, 1, heads_here, HEAD_SIZE),
        key,
        value_matrix[:, None, :],
        my_doc,
        my_pos,
    )
    return result.reshape(capacity, heads_here * HEAD_SIZE)


def fused_kernel(
    shards, capacity, heads_here,
    len_hbm, shard_hbm, slot_hbm, freq_hbm, tokens_hbm, wq_hbm, wk_hbm, wv_hbm, out_ref,
    len_ref, shard_ref, slot_ref, freq_ref, tok, weights, place, work, inbox, total_buf, term_buf,
    key_buf, value_buf, cos_buf, sin_buf, first_buf, mask_buf,
    table_sem, piece_sem, w_sem, send_sem, recv_sem,
):
    bits = shards.bit_length() - 1
    chunks = heads_here // 2 + 1
    groups = heads_here // 4 + 1
    wide = 4 * HEAD_SIZE
    tokens_total, depth = tok.shape
    pieces = piece_sem.shape[0]
    piece = depth // pieces
    documents = len_ref.shape[0]
    head = HEAD_SIZE
    lags = [2 * p - (p == bits) for p in range(bits + 1)]
    last_lag = lags[bits]
    me = lax.axis_index("ctx")
    column = lax.axis_index("tp")
    orders = [list(range(bits)), list(reversed(range(bits)))]
    inbox_at = [sum(shards >> (q + 1) for q in range(p)) * capacity for p in range(bits)]

    def peer(bit):
        step = 1 << bit
        return me + step - 2 * step * ((me // step) % 2)

    def flipped(mask):
        ident = 0
        for bit in range(bits):
            own = (me // (1 << bit)) % 2
            ident = ident + ((1 - own) if (mask >> bit) & 1 else own) * (1 << bit)
        return ident

    def mask_at(order, spot):
        mask = 0
        for p, bit in enumerate(order):
            if (spot >> (bits - 1 - p)) & 1:
                mask |= 1 << bit
        return mask

    tables = [
        pltpu.make_async_copy(source, target, table_sem.at[i])
        for i, (source, target) in enumerate(
            [(len_hbm, len_ref), (shard_hbm, shard_ref), (slot_hbm, slot_ref), (freq_hbm, freq_ref)]
        )
    ]

    def load_piece(k):
        part = pl.ds(k * piece, piece)
        return [
            pltpu.make_async_copy(tokens_hbm.at[:, part], tok.at[:, part], piece_sem.at[k, 0]),
            pltpu.make_async_copy(
                wk_hbm.at[part], weights.at[0, part, pl.ds(0, head)], piece_sem.at[k, 1]
            ),
            pltpu.make_async_copy(
                wv_hbm.at[part], weights.at[0, part, pl.ds(head, head)], piece_sem.at[k, 2]
            ),
        ]

    def load_query(g):
        at = pl.multiple_of((g - 1) * wide, wide)
        return pltpu.make_async_copy(wq_hbm.at[:, pl.ds(at, wide)], weights.at[g], w_sem.at[g])

    def send(c, half, p):
        rows = (shards >> (p + 1)) * capacity
        return pltpu.make_async_remote_copy(
            src_ref=work.at[c, half, pl.ds(rows, rows)],
            dst_ref=inbox.at[c, half, pl.ds(inbox_at[p], rows)],
            send_sem=send_sem.at[c, half, p],
            recv_sem=recv_sem.at[c, half, p],
            device_id=(peer(orders[half][p]), column),
            device_id_type=pl.DeviceIdType.MESH,
        )

    for copy in tables:
        copy.start()
    for k in range(pieces):
        for copy in load_piece(k):
            copy.start()

    barrier = pltpu.get_barrier_semaphore()
    for bit in range(bits):
        pl.semaphore_signal(
            barrier, inc=1, device_id=(peer(bit), column), device_id_type=pl.DeviceIdType.MESH
        )

    token_ids = lax.broadcasted_iota(jnp.int32, (1, tokens_total), 1)
    slot_ids = lax.broadcasted_iota(jnp.int32, (capacity, head), 0)

    for copy in tables:
        copy.wait()

    def place_document(d, carry):
        start, target = carry
        length = len_ref[d]
        anchor = shard_ref[d] * capacity + slot_ref[d]
        inside = (token_ids >= start) & (token_ids < start + length)
        target = jnp.where(inside, anchor + token_ids - start, target)
        return start + length, target

    _, target = lax.fori_loop(
        0, documents, place_document, (jnp.int32(0), jnp.zeros_like(token_ids))
    )

    def build_place():
        local = lax.broadcasted_iota(jnp.int32, (capacity, tokens_total), 0)
        for mask in range(shards):
            hit = local == target - flipped(mask) * capacity
            place[pl.ds(mask * capacity, capacity), :] = jnp.where(hit, 1.0, 0.0).astype(
                jnp.bfloat16
            )

    def first_slot(d, first):
        slot = slot_ref[d]
        here = jnp.where(shard_ref[d] == me, len_ref[d], 0)
        return jnp.where((slot_ids >= slot) & (slot_ids < slot + here), slot, first)

    def first_product():
        for k in range(pieces):
            if k == pieces - 1:
                load_query(1).start()
                build_place()
            for copy in load_piece(k):
                copy.wait()
            part = pl.ds(k * piece, piece)
            term = jnp.dot(
                tok[:, part], weights[0, part, : 2 * head], preferred_element_type=jnp.float32
            )
            if k > 0:
                term = total_buf[...] + term
            if k < pieces - 1:
                total_buf[...] = term
        term_buf[1] = term.astype(jnp.bfloat16)
        pl.semaphore_wait(barrier, bits)

    def product(g):
        load_query(g).wait()
        term = jnp.dot(tok[...], weights[g], preferred_element_type=jnp.float32)
        term = term.astype(jnp.bfloat16)
        term_buf[0] = term[:, : 2 * head]
        term_buf[1] = term[:, 2 * head :]

    def produce(c):
        placed = jnp.dot(
            place[...], term_buf[(c + 1) % 2], preferred_element_type=jnp.float32
        )
        placed = placed.astype(jnp.bfloat16)
        for half in range(2):
            for spot in reversed(range(shards)):
                mask = mask_at(orders[half], spot)
                work[c, half, pl.ds(spot * capacity, capacity), :] = placed[
                    mask * capacity : (mask + 1) * capacity, half * head : (half + 1) * head
                ]
        for half in range(2):
            send(c, half, 0).start()

    def gathered(c, half, spot, phases):
        value = work[c, half, pl.ds(spot * capacity, capacity), :].astype(jnp.float32)
        for p in range(phases):
            value = value + inbox[
                c, half, pl.ds(inbox_at[p] + spot * capacity, capacity), :
            ].astype(jnp.float32)
        return value

    def relay(c, p):
        for half in range(2):
            send(c, half, p - 1).wait_recv()
            for spot in range(shards >> (p + 1), shards >> p):
                work[c, half, pl.ds(spot * capacity, capacity), :] = gathered(
                    c, half, spot, p
                ).astype(jnp.bfloat16)
            send(c, half, p).start()

    def rotate(value):
        return value * cos_buf[...] + pltpu.roll(value, head // 2, 1) * sin_buf[...]

    def take_key_value():
        wait_last(0)
        first = lax.fori_loop(0, documents, first_slot, slot_ids)
        first_buf[...] = first
        angle = (slot_ids - first).astype(jnp.float32) * freq_ref[...]
        lane = lax.broadcasted_iota(jnp.int32, (capacity, head), 1)
        cos_buf[...] = jnp.cos(angle)
        sine = jnp.sin(angle)
        sin_buf[...] = jnp.where(lane < head // 2, -sine, sine)
        key_raw = gathered(0, 0, 0, bits).astype(jnp.bfloat16).astype(jnp.float32)
        key_buf[...] = rotate(key_raw).astype(jnp.bfloat16)
        value_buf[...] = gathered(0, 1, 0, bits).astype(jnp.bfloat16)
        row = lax.broadcasted_iota(jnp.int32, (capacity, capacity), 0)
        col = lax.broadcasted_iota(jnp.int32, (capacity, capacity), 1)
        allowed = (col <= row) & (col >= first_buf[:, :1])
        mask_buf[...] = jnp.where(allowed, 0.0, -jnp.inf)

    def attend_heads(c):
        query = [rotate(gathered(c, half, 0, bits)).astype(jnp.bfloat16) for half in range(2)]
        scores = lax.dot_general(
            jnp.concatenate(query, axis=0),
            key_buf[...],
            (((1,), (1,)), ((), ())),
            preferred_element_type=jnp.float32,
        )
        scores = scores + jnp.concatenate([mask_buf[...], mask_buf[...]], axis=0)
        peak = jnp.max(scores, axis=-1, keepdims=True)
        expo = jnp.exp2((scores - peak) * (head**-0.5 * np.log2(np.e)))
        total = jnp.sum(expo, axis=-1, keepdims=True)
        mixed = jnp.dot(
            expo.astype(jnp.bfloat16), value_buf[...], preferred_element_type=jnp.float32
        )
        result = (mixed / total).astype(jnp.bfloat16)
        for half in range(2):
            at = pl.multiple_of((c - 1) * (2 * head) + half * head, head)
            out_ref[:, pl.ds(at, head)] = result[half * capacity : (half + 1) * capacity]

    def wait_last(c):
        for half in range(2):
            send(c, half, bits - 1).wait_recv()

    def step(c, _):
        @pl.when(c == 0)
        def _():
            first_product()

        @pl.when((c % 2 == 1) & (c < chunks))
        def _():
            product((c + 1) // 2)

        @pl.when((c % 2 == 1) & ((c + 1) // 2 + 1 < groups))
        def _():
            load_query((c + 1) // 2 + 1).start()

        @pl.when(c < chunks)
        def _():
            produce(c)

        for p in range(1, bits):
            @pl.when((c >= lags[p]) & (c < chunks + lags[p]))
            def _():
                relay(c - lags[p], p)

        @pl.when(c == last_lag)
        def _():
            take_key_value()

        @pl.when(c > last_lag)
        def _():
            wait_last(c - last_lag)
            attend_heads(c - last_lag)

        return 0

    lax.fori_loop(0, chunks + last_lag, step, 0)

    def finish(c, _):
        for half in range(2):
            for p in range(bits):
                send(c, half, p).wait_send()
        return 0

    lax.fori_loop(0, chunks, finish, 0)


def fused(tokens, wq, wk, wv, doc_len, doc_shard, doc_slot):
    shards = lax.axis_size("ctx")
    bits = shards.bit_length() - 1
    total_tokens, depth = tokens.shape
    per_shard = total_tokens // shards
    capacity = per_shard + per_shard // 2
    q_cols = wq.shape[1]
    heads_here = q_cols // HEAD_SIZE
    chunks = heads_here // 2 + 1
    groups = heads_here // 4 + 1
    half = HEAD_SIZE // 2
    freq = np.power(np.float32(rope_base), -np.arange(half, dtype=np.float32) * np.float32(2.0 / HEAD_SIZE))
    freq = jnp.asarray(np.tile(freq, 2)[None, :], jnp.float32)
    documents = doc_len.shape[0]
    hbm = pl.BlockSpec(memory_space=pl.ANY)
    bf16 = jnp.bfloat16
    return pl.pallas_call(
        functools.partial(fused_kernel, shards, capacity, heads_here),
        out_shape=pltpu.VMEM((capacity, q_cols), bf16),
        in_specs=[hbm] * 8,
        out_specs=pl.BlockSpec(memory_space=pltpu.VMEM),
        scratch_shapes=[
            pltpu.SMEM((documents,), jnp.int32),
            pltpu.SMEM((documents,), jnp.int32),
            pltpu.SMEM((documents,), jnp.int32),
            pltpu.VMEM((1, HEAD_SIZE), jnp.float32),
            pltpu.VMEM((total_tokens, depth), bf16),
            pltpu.VMEM((groups, depth, 4 * HEAD_SIZE), bf16),
            pltpu.VMEM((shards * capacity, total_tokens), bf16),
            pltpu.VMEM((chunks, 2, shards * capacity, HEAD_SIZE), bf16),
            pltpu.VMEM((chunks, 2, (shards - 1) * capacity, HEAD_SIZE), bf16),
            pltpu.VMEM((total_tokens, 2 * HEAD_SIZE), jnp.float32),
            pltpu.VMEM((2, total_tokens, 2 * HEAD_SIZE), bf16),
            pltpu.VMEM((capacity, HEAD_SIZE), bf16),
            pltpu.VMEM((capacity, HEAD_SIZE), bf16),
            pltpu.VMEM((capacity, HEAD_SIZE), jnp.float32),
            pltpu.VMEM((capacity, HEAD_SIZE), jnp.float32),
            pltpu.VMEM((capacity, HEAD_SIZE), jnp.int32),
            pltpu.VMEM((capacity, capacity), jnp.float32),
            pltpu.SemaphoreType.DMA((4,)),
            pltpu.SemaphoreType.DMA((4, 3)),
            pltpu.SemaphoreType.DMA((groups,)),
            pltpu.SemaphoreType.DMA((chunks, 2, bits)),
            pltpu.SemaphoreType.DMA((chunks, 2, bits)),
        ],
        compiler_params=pltpu.CompilerParams(
            collective_id=0, has_side_effects=True, vmem_limit_bytes=56 * 2**20
        ),
        cost_estimate=pl.CostEstimate(
            flops=2 * total_tokens * depth * (q_cols + 2 * HEAD_SIZE),
            bytes_accessed=2 * depth * (total_tokens + q_cols + 2 * HEAD_SIZE),
            transcendentals=0,
        ),
    )(doc_len, doc_shard, doc_slot, freq, tokens, wq, wk, wv)


def body(tokens, wq, wk, wv, doc_len, doc_shard, doc_slot):
    shards = lax.axis_size("ctx")
    whole_groups = wq.shape[1] % (4 * HEAD_SIZE) == 0
    if wk.shape[1] == HEAD_SIZE and shards & (shards - 1) == 0 and whole_groups:
        return fused(tokens, wq, wk, wv, doc_len, doc_shard, doc_slot)
    return plain(tokens, wq, wk, wv, doc_len, doc_shard, doc_slot)


def solution(mesh):
    return jax.shard_map(
        body,
        mesh=mesh,
        in_specs=(P(None, "ctx"), P("ctx", "tp"), P("ctx", "tp"), P("ctx", "tp"), P(), P(), P()),
        out_specs=P("ctx", "tp"),
        check_vma=False,
    )
```

```python
import functools

import jax
import jax.numpy as jnp
import numpy as np
from jax import lax
from jax.experimental import pallas as pl
from jax.experimental.pallas import tpu as pltpu
from jax.sharding import PartitionSpec as P

HEAD_SIZE = 128


rope_base = 500000.0


def partner(shard, axis, apart):
    return lax.ppermute(shard, axis, [(i, i ^ 1 << apart) for i in range(lax.axis_size(axis))])


def slot_layout(doc_len, doc_shard, doc_slot, tokens_total, capacity, slot_total):
    ends = jnp.cumsum(doc_len)
    starts = ends - doc_len
    token_ids = jnp.arange(tokens_total, dtype=jnp.int32)
    inside = (token_ids[:, None] >= starts[None, :]) & (token_ids[:, None] < ends[None, :])
    doc_ids = jnp.arange(doc_len.shape[0], dtype=jnp.int32)
    doc_of = jnp.sum(jnp.where(inside, doc_ids[None, :], 0), axis=1)
    first = jnp.sum(jnp.where(inside, starts[None, :], 0), axis=1)
    anchor = doc_shard * capacity + doc_slot
    base = jnp.sum(jnp.where(inside, anchor[None, :], 0), axis=1)
    position = token_ids - first
    target = base + position
    slot_ids = jnp.arange(slot_total, dtype=jnp.int32)
    source = jnp.zeros((slot_total,), jnp.int32).at[target].set(token_ids)
    filled = jnp.zeros((slot_total,), jnp.int32).at[target].set(1)
    slot_doc = jnp.zeros((slot_total,), jnp.int32).at[target].set(doc_of)
    slot_doc = jnp.where(filled == 1, slot_doc, -1 - slot_ids)
    slot_position_index = jnp.zeros((slot_total,), jnp.int32).at[target].set(position)
    return (source, filled, slot_doc, slot_position_index)


def apply_rotary(values, positions):
    head_dim = values.shape[-1]
    half = head_dim // 2
    freq = jnp.power(
        jnp.float32(rope_base), -jnp.arange(half, dtype=jnp.float32) * (2.0 / head_dim)
    )
    angle = positions.astype(jnp.float32)[:, None] * freq[None, :]
    cosine = jnp.cos(angle)[:, None, :]
    sine = jnp.sin(angle)[:, None, :]
    lower = values[..., :half]
    upper = values[..., half:]
    return jnp.concatenate([lower * cosine - upper * sine, upper * cosine + lower * sine], axis=-1)


def attend(query_matrix, key, value_matrix, slot_doc, slot_position_index):
    scale = query_matrix.shape[-1] ** (-0.5)
    scores = (
        jnp.einsum("qgjd,kgd->gjqk", query_matrix, key, preferred_element_type=jnp.float32) * scale
    )
    allowed = (slot_doc[:, None] == slot_doc[None, :]) & (
        slot_position_index[None, :] <= slot_position_index[:, None]
    )
    scores = jnp.where(allowed[None, None], scores, -jnp.inf)
    peak = jnp.max(scores, axis=-1, keepdims=True)
    expo = jnp.exp(scores - peak)
    total = jnp.sum(expo, axis=-1)
    weights = expo.astype(jnp.bfloat16)
    mixed = jnp.einsum("gjqk,kgd->qgjd", weights, value_matrix, preferred_element_type=jnp.float32)
    result = mixed / jnp.transpose(total, (2, 0, 1))[..., None]
    return result.astype(jnp.bfloat16)


def plain(tokens, wq, wk, wv, doc_len, doc_shard, doc_slot):
    shards = lax.axis_size("ctx")
    total_tokens = tokens.shape[0]
    per_shard = total_tokens // shards
    capacity = per_shard + per_shard // 2
    slot_total = capacity * shards
    source, filled, slot_doc, slot_position_index = slot_layout(
        doc_len, doc_shard, doc_slot, total_tokens, capacity, slot_total
    )
    joined = jnp.concatenate([wq, wk, wv], axis=1)
    q_cols = wq.shape[1]
    key_value_columns = wk.shape[1]
    picked = jnp.take(tokens, source, axis=0)
    partial_rows = jnp.dot(picked, joined, preferred_element_type=jnp.float32)
    summed = lax.psum_scatter(
        jnp.where(filled[:, None] == 1, partial_rows, jnp.float32(0.0)).astype(jnp.bfloat16),
        "ctx",
        scatter_dimension=0,
        tiled=True,
    ).astype(jnp.float32)
    shard = lax.axis_index("ctx")
    my_doc = lax.dynamic_slice_in_dim(slot_doc, shard * capacity, capacity)
    my_pos = lax.dynamic_slice_in_dim(slot_position_index, shard * capacity, capacity)
    heads_here = q_cols // HEAD_SIZE
    query_matrix = apply_rotary(
        summed[:, :q_cols].reshape(capacity, heads_here, HEAD_SIZE), my_pos
    ).astype(jnp.bfloat16)
    piece = jnp.stack(
        [summed[:, q_cols : q_cols + key_value_columns], summed[:, q_cols + key_value_columns :]],
        axis=0,
    ).astype(jnp.bfloat16)
    members = HEAD_SIZE // key_value_columns
    member = lax.axis_index("tp") % members
    for bit in range(members.bit_length() - 1):
        other = partner(piece, "tp", bit)
        upper_bit = member // 2**bit % 2
        lower_part = jnp.where(upper_bit == 0, piece, other)
        upper_part = jnp.where(upper_bit == 0, other, piece)
        piece = jnp.concatenate([lower_part, upper_part], axis=2)
    key_unrotated = lax.optimization_barrier(piece[0])
    value_matrix = piece[1]
    key = apply_rotary(key_unrotated.astype(jnp.float32)[:, None, :], my_pos).astype(jnp.bfloat16)
    result = attend(
        query_matrix.reshape(capacity, 1, heads_here, HEAD_SIZE),
        key,
        value_matrix[:, None, :],
        my_doc,
        my_pos,
    )
    return result.reshape(capacity, heads_here * HEAD_SIZE)


def fused_kernel(
    shards, capacity, heads_here,
    len_hbm, shard_hbm, slot_hbm, freq_hbm, tokens_hbm, wq_hbm, wk_hbm, wv_hbm, out_ref,
    len_ref, shard_ref, slot_ref, freq_ref, tok, weights, place, work, inbox, total_buf, term_buf,
    key_buf, value_buf, cos_buf, sin_buf, first_buf, mask_buf,
    table_sem, piece_sem, w_sem, send_sem, recv_sem,
):
    bits = shards.bit_length() - 1
    chunks = heads_here // 2 + 1
    tokens_total, depth = tok.shape
    pieces = piece_sem.shape[0]
    piece = depth // pieces
    documents = len_ref.shape[0]
    head = HEAD_SIZE
    lags = [2 * p for p in range(bits + 1)]
    last_lag = lags[bits]
    me = lax.axis_index("ctx")
    column = lax.axis_index("tp")
    orders = [list(range(bits)), list(reversed(range(bits)))]
    inbox_at = [sum(shards >> (q + 1) for q in range(p)) * capacity for p in range(bits)]

    def peer(bit):
        step = 1 << bit
        return me + step - 2 * step * ((me // step) % 2)

    def flipped(mask):
        ident = 0
        for bit in range(bits):
            own = (me // (1 << bit)) % 2
            ident = ident + ((1 - own) if (mask >> bit) & 1 else own) * (1 << bit)
        return ident

    def mask_at(order, spot):
        mask = 0
        for p, bit in enumerate(order):
            if (spot >> (bits - 1 - p)) & 1:
                mask |= 1 << bit
        return mask

    tables = [
        pltpu.make_async_copy(source, target, table_sem.at[i])
        for i, (source, target) in enumerate(
            [(len_hbm, len_ref), (shard_hbm, shard_ref), (slot_hbm, slot_ref), (freq_hbm, freq_ref)]
        )
    ]

    def load_piece(k):
        part = pl.ds(k * piece, piece)
        return [
            pltpu.make_async_copy(tokens_hbm.at[:, part], tok.at[:, part], piece_sem.at[k, 0]),
            pltpu.make_async_copy(
                wk_hbm.at[part], weights.at[0, part, pl.ds(0, head)], piece_sem.at[k, 1]
            ),
            pltpu.make_async_copy(
                wv_hbm.at[part], weights.at[0, part, pl.ds(head, head)], piece_sem.at[k, 2]
            ),
        ]

    def load_query(c):
        at = pl.multiple_of((c - 1) * (2 * head), 2 * head)
        return pltpu.make_async_copy(
            wq_hbm.at[:, pl.ds(at, 2 * head)], weights.at[c], w_sem.at[c]
        )

    def send(c, half, p):
        rows = (shards >> (p + 1)) * capacity
        return pltpu.make_async_remote_copy(
            src_ref=work.at[c, half, pl.ds(rows, rows)],
            dst_ref=inbox.at[c, half, pl.ds(inbox_at[p], rows)],
            send_sem=send_sem.at[c, half, p],
            recv_sem=recv_sem.at[c, half, p],
            device_id=(peer(orders[half][p]), column),
            device_id_type=pl.DeviceIdType.MESH,
        )

    for copy in tables:
        copy.start()
    for k in range(pieces):
        for copy in load_piece(k):
            copy.start()

    barrier = pltpu.get_barrier_semaphore()
    for bit in range(bits):
        pl.semaphore_signal(
            barrier, inc=1, device_id=(peer(bit), column), device_id_type=pl.DeviceIdType.MESH
        )

    token_ids = lax.broadcasted_iota(jnp.int32, (1, tokens_total), 1)
    slot_ids = lax.broadcasted_iota(jnp.int32, (capacity, head), 0)

    for copy in tables:
        copy.wait()

    def place_document(d, carry):
        start, target = carry
        length = len_ref[d]
        anchor = shard_ref[d] * capacity + slot_ref[d]
        inside = (token_ids >= start) & (token_ids < start + length)
        target = jnp.where(inside, anchor + token_ids - start, target)
        return start + length, target

    _, target = lax.fori_loop(
        0, documents, place_document, (jnp.int32(0), jnp.zeros_like(token_ids))
    )

    def build_place():
        local = lax.broadcasted_iota(jnp.int32, (capacity, tokens_total), 0)
        for mask in range(shards):
            hit = local == target - flipped(mask) * capacity
            place[pl.ds(mask * capacity, capacity), :] = jnp.where(hit, 1.0, 0.0).astype(
                jnp.bfloat16
            )

    def first_slot(d, first):
        slot = slot_ref[d]
        here = jnp.where(shard_ref[d] == me, len_ref[d], 0)
        return jnp.where((slot_ids >= slot) & (slot_ids < slot + here), slot, first)

    def first_product():
        for k in range(pieces):
            if k == pieces - 1:
                load_query(1).start()
                build_place()
            for copy in load_piece(k):
                copy.wait()
            part = pl.ds(k * piece, piece)
            term = jnp.dot(
                tok[:, part], weights[0, part, :], preferred_element_type=jnp.float32
            )
            if k > 0:
                term = total_buf[...] + term
            if k < pieces - 1:
                total_buf[...] = term
        term_buf[...] = term.astype(jnp.bfloat16)
        pl.semaphore_wait(barrier, bits)

    def product(c):
        load_query(c).wait()
        term_buf[...] = jnp.dot(
            tok[...], weights[c], preferred_element_type=jnp.float32
        ).astype(jnp.bfloat16)

    def produce(c):
        placed = jnp.dot(place[...], term_buf[...], preferred_element_type=jnp.float32)
        placed = placed.astype(jnp.bfloat16)
        for half in range(2):
            for spot in reversed(range(shards)):
                mask = mask_at(orders[half], spot)
                work[c, half, pl.ds(spot * capacity, capacity), :] = placed[
                    mask * capacity : (mask + 1) * capacity, half * head : (half + 1) * head
                ]
        for half in range(2):
            send(c, half, 0).start()

    def gathered(c, half, spot, phases):
        value = work[c, half, pl.ds(spot * capacity, capacity), :].astype(jnp.float32)
        for p in range(phases):
            value = value + inbox[
                c, half, pl.ds(inbox_at[p] + spot * capacity, capacity), :
            ].astype(jnp.float32)
        return value

    def relay(c, p):
        for half in range(2):
            send(c, half, p - 1).wait_recv()
            for spot in range(shards >> (p + 1), shards >> p):
                work[c, half, pl.ds(spot * capacity, capacity), :] = gathered(
                    c, half, spot, p
                ).astype(jnp.bfloat16)
            send(c, half, p).start()

    def rotate(value):
        return value * cos_buf[...] + pltpu.roll(value, head // 2, 1) * sin_buf[...]

    def take_key_value():
        wait_last(0)
        first = lax.fori_loop(0, documents, first_slot, slot_ids)
        first_buf[...] = first
        angle = (slot_ids - first).astype(jnp.float32) * freq_ref[...]
        lane = lax.broadcasted_iota(jnp.int32, (capacity, head), 1)
        cos_buf[...] = jnp.cos(angle)
        sine = jnp.sin(angle)
        sin_buf[...] = jnp.where(lane < head // 2, -sine, sine)
        key_raw = gathered(0, 0, 0, bits).astype(jnp.bfloat16).astype(jnp.float32)
        key_buf[...] = rotate(key_raw).astype(jnp.bfloat16)
        value_buf[...] = gathered(0, 1, 0, bits).astype(jnp.bfloat16)
        row = lax.broadcasted_iota(jnp.int32, (capacity, capacity), 0)
        col = lax.broadcasted_iota(jnp.int32, (capacity, capacity), 1)
        allowed = (col <= row) & (col >= first_buf[:, :1])
        mask_buf[...] = jnp.where(allowed, 0.0, -jnp.inf)

    def attend_heads(c):
        query = [rotate(gathered(c, half, 0, bits)).astype(jnp.bfloat16) for half in range(2)]
        scores = lax.dot_general(
            jnp.concatenate(query, axis=0),
            key_buf[...],
            (((1,), (1,)), ((), ())),
            preferred_element_type=jnp.float32,
        )
        scores = scores + jnp.concatenate([mask_buf[...], mask_buf[...]], axis=0)
        peak = jnp.max(scores, axis=-1, keepdims=True)
        expo = jnp.exp2((scores - peak) * (head**-0.5 * np.log2(np.e)))
        total = jnp.sum(expo, axis=-1, keepdims=True)
        mixed = jnp.dot(
            expo.astype(jnp.bfloat16), value_buf[...], preferred_element_type=jnp.float32
        )
        result = (mixed / total).astype(jnp.bfloat16)
        for half in range(2):
            at = pl.multiple_of((c - 1) * (2 * head) + half * head, head)
            out_ref[:, pl.ds(at, head)] = result[half * capacity : (half + 1) * capacity]

    def wait_last(c):
        for half in range(2):
            send(c, half, bits - 1).wait_recv()

    def step(c, _):
        @pl.when(c == 0)
        def _():
            first_product()

        @pl.when((c > 0) & (c < chunks))
        def _():
            product(c)

        @pl.when(c + 2 < chunks)
        def _():
            load_query(c + 2).start()

        @pl.when(c < chunks)
        def _():
            produce(c)

        for p in range(1, bits):
            @pl.when((c >= lags[p]) & (c < chunks + lags[p]))
            def _():
                relay(c - lags[p], p)

        @pl.when(c == last_lag)
        def _():
            take_key_value()

        @pl.when(c > last_lag)
        def _():
            wait_last(c - last_lag)
            attend_heads(c - last_lag)

        return 0

    lax.fori_loop(0, chunks + last_lag, step, 0)

    def finish(c, _):
        for half in range(2):
            for p in range(bits):
                send(c, half, p).wait_send()
        return 0

    lax.fori_loop(0, chunks, finish, 0)


def fused(tokens, wq, wk, wv, doc_len, doc_shard, doc_slot):
    shards = lax.axis_size("ctx")
    bits = shards.bit_length() - 1
    total_tokens, depth = tokens.shape
    per_shard = total_tokens // shards
    capacity = per_shard + per_shard // 2
    q_cols = wq.shape[1]
    heads_here = q_cols // HEAD_SIZE
    chunks = heads_here // 2 + 1
    half = HEAD_SIZE // 2
    freq = np.power(np.float32(rope_base), -np.arange(half, dtype=np.float32) * np.float32(2.0 / HEAD_SIZE))
    freq = jnp.asarray(np.tile(freq, 2)[None, :], jnp.float32)
    documents = doc_len.shape[0]
    hbm = pl.BlockSpec(memory_space=pl.ANY)
    bf16 = jnp.bfloat16
    return pl.pallas_call(
        functools.partial(fused_kernel, shards, capacity, heads_here),
        out_shape=pltpu.VMEM((capacity, q_cols), bf16),
        in_specs=[hbm] * 8,
        out_specs=pl.BlockSpec(memory_space=pltpu.VMEM),
        scratch_shapes=[
            pltpu.SMEM((documents,), jnp.int32),
            pltpu.SMEM((documents,), jnp.int32),
            pltpu.SMEM((documents,), jnp.int32),
            pltpu.VMEM((1, HEAD_SIZE), jnp.float32),
            pltpu.VMEM((total_tokens, depth), bf16),
            pltpu.VMEM((chunks, depth, 2 * HEAD_SIZE), bf16),
            pltpu.VMEM((shards * capacity, total_tokens), bf16),
            pltpu.VMEM((chunks, 2, shards * capacity, HEAD_SIZE), bf16),
            pltpu.VMEM((chunks, 2, (shards - 1) * capacity, HEAD_SIZE), bf16),
            pltpu.VMEM((total_tokens, 2 * HEAD_SIZE), jnp.float32),
            pltpu.VMEM((total_tokens, 2 * HEAD_SIZE), bf16),
            pltpu.VMEM((capacity, HEAD_SIZE), bf16),
            pltpu.VMEM((capacity, HEAD_SIZE), bf16),
            pltpu.VMEM((capacity, HEAD_SIZE), jnp.float32),
            pltpu.VMEM((capacity, HEAD_SIZE), jnp.float32),
            pltpu.VMEM((capacity, HEAD_SIZE), jnp.int32),
            pltpu.VMEM((capacity, capacity), jnp.float32),
            pltpu.SemaphoreType.DMA((4,)),
            pltpu.SemaphoreType.DMA((4, 3)),
            pltpu.SemaphoreType.DMA((chunks,)),
            pltpu.SemaphoreType.DMA((chunks, 2, bits)),
            pltpu.SemaphoreType.DMA((chunks, 2, bits)),
        ],
        compiler_params=pltpu.CompilerParams(
            collective_id=0, has_side_effects=True, vmem_limit_bytes=56 * 2**20
        ),
        cost_estimate=pl.CostEstimate(
            flops=2 * total_tokens * depth * (q_cols + 2 * HEAD_SIZE),
            bytes_accessed=2 * depth * (total_tokens + q_cols + 2 * HEAD_SIZE),
            transcendentals=0,
        ),
    )(doc_len, doc_shard, doc_slot, freq, tokens, wq, wk, wv)


def body(tokens, wq, wk, wv, doc_len, doc_shard, doc_slot):
    shards = lax.axis_size("ctx")
    paired = wq.shape[1] % (2 * HEAD_SIZE) == 0
    if wk.shape[1] == HEAD_SIZE and shards & (shards - 1) == 0 and paired:
        return fused(tokens, wq, wk, wv, doc_len, doc_shard, doc_slot)
    return plain(tokens, wq, wk, wv, doc_len, doc_shard, doc_slot)


def solution(mesh):
    return jax.shard_map(
        body,
        mesh=mesh,
        in_specs=(P(None, "ctx"), P("ctx", "tp"), P("ctx", "tp"), P("ctx", "tp"), P(), P(), P()),
        out_specs=P("ctx", "tp"),
        check_vma=False,
    )
```

```python
import functools

import jax
import jax.numpy as jnp
import numpy as np
from jax import lax
from jax.experimental import pallas as pl
from jax.experimental.pallas import tpu as pltpu
from jax.sharding import PartitionSpec as P

HEAD_SIZE = 128


rope_base = 500000.0


def partner(shard, axis, apart):
    return lax.ppermute(shard, axis, [(i, i ^ 1 << apart) for i in range(lax.axis_size(axis))])


def slot_layout(doc_len, doc_shard, doc_slot, tokens_total, capacity, slot_total):
    ends = jnp.cumsum(doc_len)
    starts = ends - doc_len
    token_ids = jnp.arange(tokens_total, dtype=jnp.int32)
    inside = (token_ids[:, None] >= starts[None, :]) & (token_ids[:, None] < ends[None, :])
    doc_ids = jnp.arange(doc_len.shape[0], dtype=jnp.int32)
    doc_of = jnp.sum(jnp.where(inside, doc_ids[None, :], 0), axis=1)
    first = jnp.sum(jnp.where(inside, starts[None, :], 0), axis=1)
    anchor = doc_shard * capacity + doc_slot
    base = jnp.sum(jnp.where(inside, anchor[None, :], 0), axis=1)
    position = token_ids - first
    target = base + position
    slot_ids = jnp.arange(slot_total, dtype=jnp.int32)
    source = jnp.zeros((slot_total,), jnp.int32).at[target].set(token_ids)
    filled = jnp.zeros((slot_total,), jnp.int32).at[target].set(1)
    slot_doc = jnp.zeros((slot_total,), jnp.int32).at[target].set(doc_of)
    slot_doc = jnp.where(filled == 1, slot_doc, -1 - slot_ids)
    slot_position_index = jnp.zeros((slot_total,), jnp.int32).at[target].set(position)
    return (source, filled, slot_doc, slot_position_index)


def apply_rotary(values, positions):
    head_dim = values.shape[-1]
    half = head_dim // 2
    freq = jnp.power(
        jnp.float32(rope_base), -jnp.arange(half, dtype=jnp.float32) * (2.0 / head_dim)
    )
    angle = positions.astype(jnp.float32)[:, None] * freq[None, :]
    cosine = jnp.cos(angle)[:, None, :]
    sine = jnp.sin(angle)[:, None, :]
    lower = values[..., :half]
    upper = values[..., half:]
    return jnp.concatenate([lower * cosine - upper * sine, upper * cosine + lower * sine], axis=-1)


def attend(query_matrix, key, value_matrix, slot_doc, slot_position_index):
    scale = query_matrix.shape[-1] ** (-0.5)
    scores = (
        jnp.einsum("qgjd,kgd->gjqk", query_matrix, key, preferred_element_type=jnp.float32) * scale
    )
    allowed = (slot_doc[:, None] == slot_doc[None, :]) & (
        slot_position_index[None, :] <= slot_position_index[:, None]
    )
    scores = jnp.where(allowed[None, None], scores, -jnp.inf)
    peak = jnp.max(scores, axis=-1, keepdims=True)
    expo = jnp.exp(scores - peak)
    total = jnp.sum(expo, axis=-1)
    weights = expo.astype(jnp.bfloat16)
    mixed = jnp.einsum("gjqk,kgd->qgjd", weights, value_matrix, preferred_element_type=jnp.float32)
    result = mixed / jnp.transpose(total, (2, 0, 1))[..., None]
    return result.astype(jnp.bfloat16)


def plain(tokens, wq, wk, wv, doc_len, doc_shard, doc_slot):
    shards = lax.axis_size("ctx")
    total_tokens = tokens.shape[0]
    per_shard = total_tokens // shards
    capacity = per_shard + per_shard // 2
    slot_total = capacity * shards
    source, filled, slot_doc, slot_position_index = slot_layout(
        doc_len, doc_shard, doc_slot, total_tokens, capacity, slot_total
    )
    joined = jnp.concatenate([wq, wk, wv], axis=1)
    q_cols = wq.shape[1]
    key_value_columns = wk.shape[1]
    picked = jnp.take(tokens, source, axis=0)
    partial_rows = jnp.dot(picked, joined, preferred_element_type=jnp.float32)
    summed = lax.psum_scatter(
        jnp.where(filled[:, None] == 1, partial_rows, jnp.float32(0.0)).astype(jnp.bfloat16),
        "ctx",
        scatter_dimension=0,
        tiled=True,
    ).astype(jnp.float32)
    shard = lax.axis_index("ctx")
    my_doc = lax.dynamic_slice_in_dim(slot_doc, shard * capacity, capacity)
    my_pos = lax.dynamic_slice_in_dim(slot_position_index, shard * capacity, capacity)
    heads_here = q_cols // HEAD_SIZE
    query_matrix = apply_rotary(
        summed[:, :q_cols].reshape(capacity, heads_here, HEAD_SIZE), my_pos
    ).astype(jnp.bfloat16)
    piece = jnp.stack(
        [summed[:, q_cols : q_cols + key_value_columns], summed[:, q_cols + key_value_columns :]],
        axis=0,
    ).astype(jnp.bfloat16)
    members = HEAD_SIZE // key_value_columns
    member = lax.axis_index("tp") % members
    for bit in range(members.bit_length() - 1):
        other = partner(piece, "tp", bit)
        upper_bit = member // 2**bit % 2
        lower_part = jnp.where(upper_bit == 0, piece, other)
        upper_part = jnp.where(upper_bit == 0, other, piece)
        piece = jnp.concatenate([lower_part, upper_part], axis=2)
    key_unrotated = lax.optimization_barrier(piece[0])
    value_matrix = piece[1]
    key = apply_rotary(key_unrotated.astype(jnp.float32)[:, None, :], my_pos).astype(jnp.bfloat16)
    result = attend(
        query_matrix.reshape(capacity, 1, heads_here, HEAD_SIZE),
        key,
        value_matrix[:, None, :],
        my_doc,
        my_pos,
    )
    return result.reshape(capacity, heads_here * HEAD_SIZE)


def fused_kernel(
    shards, capacity, heads_here,
    len_hbm, shard_hbm, slot_hbm, freq_hbm, tokens_hbm, wq_hbm, wk_hbm, wv_hbm, out_ref,
    len_ref, shard_ref, slot_ref, freq_ref, tok, weights, place, work, inbox, total_buf, term_buf,
    key_buf, value_buf, cos_buf, sin_buf, first_buf, mask_buf,
    table_sem, piece_sem, w_sem, send_sem, recv_sem,
):
    bits = shards.bit_length() - 1
    chunks = heads_here // 2 + 1
    tokens_total, depth = tok.shape
    pieces = piece_sem.shape[0]
    piece = depth // pieces
    documents = len_ref.shape[0]
    head = HEAD_SIZE
    lags = [2 * p - 1 for p in range(bits + 1)]
    last_lag = lags[bits]
    me = lax.axis_index("ctx")
    column = lax.axis_index("tp")
    orders = [list(range(bits)), list(reversed(range(bits)))]
    inbox_at = [sum(shards >> (q + 1) for q in range(p)) * capacity for p in range(bits)]

    def peer(bit):
        step = 1 << bit
        return me + step - 2 * step * ((me // step) % 2)

    def flipped(mask):
        ident = 0
        for bit in range(bits):
            own = (me // (1 << bit)) % 2
            ident = ident + ((1 - own) if (mask >> bit) & 1 else own) * (1 << bit)
        return ident

    def mask_at(order, spot):
        mask = 0
        for p, bit in enumerate(order):
            if (spot >> (bits - 1 - p)) & 1:
                mask |= 1 << bit
        return mask

    tables = [
        pltpu.make_async_copy(source, target, table_sem.at[i])
        for i, (source, target) in enumerate(
            [(len_hbm, len_ref), (shard_hbm, shard_ref), (slot_hbm, slot_ref), (freq_hbm, freq_ref)]
        )
    ]

    def load_piece(k):
        part = pl.ds(k * piece, piece)
        return [
            pltpu.make_async_copy(tokens_hbm.at[:, part], tok.at[:, part], piece_sem.at[k, 0]),
            pltpu.make_async_copy(
                wk_hbm.at[part], weights.at[0, part, pl.ds(0, head)], piece_sem.at[k, 1]
            ),
            pltpu.make_async_copy(
                wv_hbm.at[part], weights.at[0, part, pl.ds(head, head)], piece_sem.at[k, 2]
            ),
        ]

    def load_query(c):
        at = pl.multiple_of((c - 1) * (2 * head), 2 * head)
        return pltpu.make_async_copy(
            wq_hbm.at[:, pl.ds(at, 2 * head)], weights.at[c], w_sem.at[c]
        )

    def send(c, half, p):
        rows = (shards >> (p + 1)) * capacity
        return pltpu.make_async_remote_copy(
            src_ref=work.at[c, half, pl.ds(rows, rows)],
            dst_ref=inbox.at[c, half, pl.ds(inbox_at[p], rows)],
            send_sem=send_sem.at[c, half, p],
            recv_sem=recv_sem.at[c, half, p],
            device_id=(peer(orders[half][p]), column),
            device_id_type=pl.DeviceIdType.MESH,
        )

    for copy in tables:
        copy.start()
    for k in range(pieces):
        for copy in load_piece(k):
            copy.start()

    barrier = pltpu.get_barrier_semaphore()
    for bit in range(bits):
        pl.semaphore_signal(
            barrier, inc=1, device_id=(peer(bit), column), device_id_type=pl.DeviceIdType.MESH
        )

    token_ids = lax.broadcasted_iota(jnp.int32, (1, tokens_total), 1)
    slot_ids = lax.broadcasted_iota(jnp.int32, (capacity, head), 0)

    for copy in tables:
        copy.wait()

    def place_document(d, carry):
        start, target = carry
        length = len_ref[d]
        anchor = shard_ref[d] * capacity + slot_ref[d]
        inside = (token_ids >= start) & (token_ids < start + length)
        target = jnp.where(inside, anchor + token_ids - start, target)
        return start + length, target

    _, target = lax.fori_loop(
        0, documents, place_document, (jnp.int32(0), jnp.zeros_like(token_ids))
    )

    def build_place():
        local = lax.broadcasted_iota(jnp.int32, (capacity, tokens_total), 0)
        for mask in range(shards):
            hit = local == target - flipped(mask) * capacity
            place[pl.ds(mask * capacity, capacity), :] = jnp.where(hit, 1.0, 0.0).astype(
                jnp.bfloat16
            )

    def first_slot(d, first):
        slot = slot_ref[d]
        here = jnp.where(shard_ref[d] == me, len_ref[d], 0)
        return jnp.where((slot_ids >= slot) & (slot_ids < slot + here), slot, first)

    def first_product():
        for k in range(pieces):
            if k == pieces - 1:
                load_query(1).start()
                build_place()
            for copy in load_piece(k):
                copy.wait()
            part = pl.ds(k * piece, piece)
            term = jnp.dot(
                tok[:, part], weights[0, part, :], preferred_element_type=jnp.float32
            )
            if k > 0:
                term = total_buf[...] + term
            if k < pieces - 1:
                total_buf[...] = term
        term_buf[...] = term.astype(jnp.bfloat16)
        pl.semaphore_wait(barrier, bits)

    def product(c):
        load_query(c).wait()
        term_buf[...] = jnp.dot(
            tok[...], weights[c], preferred_element_type=jnp.float32
        ).astype(jnp.bfloat16)

    def produce(c):
        placed = jnp.dot(place[...], term_buf[...], preferred_element_type=jnp.float32)
        placed = placed.astype(jnp.bfloat16)
        for half in range(2):
            for spot in reversed(range(shards)):
                mask = mask_at(orders[half], spot)
                work[c, half, pl.ds(spot * capacity, capacity), :] = placed[
                    mask * capacity : (mask + 1) * capacity, half * head : (half + 1) * head
                ]
        for half in range(2):
            send(c, half, 0).start()

    def gathered(c, half, spot, phases):
        value = work[c, half, pl.ds(spot * capacity, capacity), :].astype(jnp.float32)
        for p in range(phases):
            value = value + inbox[
                c, half, pl.ds(inbox_at[p] + spot * capacity, capacity), :
            ].astype(jnp.float32)
        return value

    def relay(c, p):
        for half in range(2):
            send(c, half, p - 1).wait_recv()
            for spot in range(shards >> (p + 1), shards >> p):
                work[c, half, pl.ds(spot * capacity, capacity), :] = gathered(
                    c, half, spot, p
                ).astype(jnp.bfloat16)
            send(c, half, p).start()

    def rotate(value):
        return value * cos_buf[...] + pltpu.roll(value, head // 2, 1) * sin_buf[...]

    def take_key_value():
        wait_last(0)
        first = lax.fori_loop(0, documents, first_slot, slot_ids)
        first_buf[...] = first
        angle = (slot_ids - first).astype(jnp.float32) * freq_ref[...]
        lane = lax.broadcasted_iota(jnp.int32, (capacity, head), 1)
        cos_buf[...] = jnp.cos(angle)
        sine = jnp.sin(angle)
        sin_buf[...] = jnp.where(lane < head // 2, -sine, sine)
        key_raw = gathered(0, 0, 0, bits).astype(jnp.bfloat16).astype(jnp.float32)
        key_buf[...] = rotate(key_raw).astype(jnp.bfloat16)
        value_buf[...] = gathered(0, 1, 0, bits).astype(jnp.bfloat16)
        row = lax.broadcasted_iota(jnp.int32, (capacity, capacity), 0)
        col = lax.broadcasted_iota(jnp.int32, (capacity, capacity), 1)
        allowed = (col <= row) & (col >= first_buf[:, :1])
        mask_buf[...] = jnp.where(allowed, 0.0, -jnp.inf)

    def attend_heads(c):
        query = [rotate(gathered(c, half, 0, bits)).astype(jnp.bfloat16) for half in range(2)]
        scores = lax.dot_general(
            jnp.concatenate(query, axis=0),
            key_buf[...],
            (((1,), (1,)), ((), ())),
            preferred_element_type=jnp.float32,
        )
        scores = scores + jnp.concatenate([mask_buf[...], mask_buf[...]], axis=0)
        peak = jnp.max(scores, axis=-1, keepdims=True)
        expo = jnp.exp2((scores - peak) * (head**-0.5 * np.log2(np.e)))
        total = jnp.sum(expo, axis=-1, keepdims=True)
        mixed = jnp.dot(
            expo.astype(jnp.bfloat16), value_buf[...], preferred_element_type=jnp.float32
        )
        result = (mixed / total).astype(jnp.bfloat16)
        for half in range(2):
            at = pl.multiple_of((c - 1) * (2 * head) + half * head, head)
            out_ref[:, pl.ds(at, head)] = result[half * capacity : (half + 1) * capacity]

    def wait_last(c):
        for half in range(2):
            send(c, half, bits - 1).wait_recv()

    def step(c, _):
        @pl.when(c == 0)
        def _():
            first_product()

        @pl.when((c > 0) & (c < chunks))
        def _():
            product(c)

        @pl.when(c + 2 < chunks)
        def _():
            load_query(c + 2).start()

        @pl.when(c < chunks)
        def _():
            produce(c)

        for p in range(1, bits):
            @pl.when((c >= lags[p]) & (c < chunks + lags[p]))
            def _():
                relay(c - lags[p], p)

        @pl.when(c == last_lag)
        def _():
            take_key_value()

        @pl.when(c > last_lag)
        def _():
            wait_last(c - last_lag)
            attend_heads(c - last_lag)

        return 0

    lax.fori_loop(0, chunks + last_lag, step, 0)

    def finish(c, _):
        for half in range(2):
            for p in range(bits):
                send(c, half, p).wait_send()
        return 0

    lax.fori_loop(0, chunks, finish, 0)


def fused(tokens, wq, wk, wv, doc_len, doc_shard, doc_slot):
    shards = lax.axis_size("ctx")
    bits = shards.bit_length() - 1
    total_tokens, depth = tokens.shape
    per_shard = total_tokens // shards
    capacity = per_shard + per_shard // 2
    q_cols = wq.shape[1]
    heads_here = q_cols // HEAD_SIZE
    chunks = heads_here // 2 + 1
    half = HEAD_SIZE // 2
    freq = np.power(np.float32(rope_base), -np.arange(half, dtype=np.float32) * np.float32(2.0 / HEAD_SIZE))
    freq = jnp.asarray(np.tile(freq, 2)[None, :], jnp.float32)
    documents = doc_len.shape[0]
    hbm = pl.BlockSpec(memory_space=pl.ANY)
    bf16 = jnp.bfloat16
    return pl.pallas_call(
        functools.partial(fused_kernel, shards, capacity, heads_here),
        out_shape=pltpu.VMEM((capacity, q_cols), bf16),
        in_specs=[hbm] * 8,
        out_specs=pl.BlockSpec(memory_space=pltpu.VMEM),
        scratch_shapes=[
            pltpu.SMEM((documents,), jnp.int32),
            pltpu.SMEM((documents,), jnp.int32),
            pltpu.SMEM((documents,), jnp.int32),
            pltpu.VMEM((1, HEAD_SIZE), jnp.float32),
            pltpu.VMEM((total_tokens, depth), bf16),
            pltpu.VMEM((chunks, depth, 2 * HEAD_SIZE), bf16),
            pltpu.VMEM((shards * capacity, total_tokens), bf16),
            pltpu.VMEM((chunks, 2, shards * capacity, HEAD_SIZE), bf16),
            pltpu.VMEM((chunks, 2, (shards - 1) * capacity, HEAD_SIZE), bf16),
            pltpu.VMEM((total_tokens, 2 * HEAD_SIZE), jnp.float32),
            pltpu.VMEM((total_tokens, 2 * HEAD_SIZE), bf16),
            pltpu.VMEM((capacity, HEAD_SIZE), bf16),
            pltpu.VMEM((capacity, HEAD_SIZE), bf16),
            pltpu.VMEM((capacity, HEAD_SIZE), jnp.float32),
            pltpu.VMEM((capacity, HEAD_SIZE), jnp.float32),
            pltpu.VMEM((capacity, HEAD_SIZE), jnp.int32),
            pltpu.VMEM((capacity, capacity), jnp.float32),
            pltpu.SemaphoreType.DMA((4,)),
            pltpu.SemaphoreType.DMA((4, 3)),
            pltpu.SemaphoreType.DMA((chunks,)),
            pltpu.SemaphoreType.DMA((chunks, 2, bits)),
            pltpu.SemaphoreType.DMA((chunks, 2, bits)),
        ],
        compiler_params=pltpu.CompilerParams(
            collective_id=0, has_side_effects=True, vmem_limit_bytes=56 * 2**20
        ),
        cost_estimate=pl.CostEstimate(
            flops=2 * total_tokens * depth * (q_cols + 2 * HEAD_SIZE),
            bytes_accessed=2 * depth * (total_tokens + q_cols + 2 * HEAD_SIZE),
            transcendentals=0,
        ),
    )(doc_len, doc_shard, doc_slot, freq, tokens, wq, wk, wv)


def body(tokens, wq, wk, wv, doc_len, doc_shard, doc_slot):
    shards = lax.axis_size("ctx")
    paired = wq.shape[1] % (2 * HEAD_SIZE) == 0
    if wk.shape[1] == HEAD_SIZE and shards & (shards - 1) == 0 and paired:
        return fused(tokens, wq, wk, wv, doc_len, doc_shard, doc_slot)
    return plain(tokens, wq, wk, wv, doc_len, doc_shard, doc_slot)


def solution(mesh):
    return jax.shard_map(
        body,
        mesh=mesh,
        in_specs=(P(None, "ctx"), P("ctx", "tp"), P("ctx", "tp"), P("ctx", "tp"), P(), P(), P()),
        out_specs=P("ctx", "tp"),
        check_vma=False,
    )
```
